32 devices in a mesh: genome: 8 (over z, x), people: 4 (over y, core).
Axes of the slice: x: 2, y: 2, z: 4, core: 2. Of those that a mesh axis runs over, the one named last changes fastest.
Arguments:
- dosages: float32 [6144, 8192], P('genome', 'people'), may hold values from 0 to 2
- annotations: int32 [6144, 128], P('genome'), may hold values from -1 to 1
Outputs:
- ld_scores: float32 [6144, 128], P(('genome', 'people'))
The draws below stay inside these ranges and needn't reach their ends.
All inputs are finite; a program needn't handle non-finite values.
Results may differ from the reference program's by a relative error of at most 0.0003.
Values sent between devices are 32-bit elements; how exact they have to be, the bound alone decides.
No kernel may reach another device: no remote copies, remote signals or barrier semaphores. Data moves between devices by JAX's collectives and lax.ppermute only.
A program may use at most 64 MiB of HBM per device.

```python
import jax
import jax.numpy as jnp
from jax import lax

B = 768
K = 128
VARIANTS = 6144
PEOPLE = 8192


def draw_dosages(key, part):
    key = jax.random.fold_in(key, 1)
    keys = jax.random.split(key, 5)
    segments = VARIANTS // (2 * B) + 2
    position = jnp.arange(VARIANTS, dtype=jnp.int32)
    first_seg = position // (2 * B)
    second_seg = (position + B) // (2 * B)
    factor_one = jax.random.normal(keys[0], (segments, PEOPLE), jnp.float32)
    factor_two = jax.random.normal(keys[1], (segments, PEOPLE), jnp.float32)
    load_one = jax.random.uniform(keys[2], (VARIANTS, 1), jnp.float32, -1.0, 1.0)
    load_two = jax.random.uniform(keys[3], (VARIANTS, 1), jnp.float32, -1.0, 1.0)
    noise = 0.3 * jax.random.normal(keys[4], (VARIANTS, PEOPLE), jnp.float32)
    signal = load_one * factor_one[first_seg] + load_two * factor_two[second_seg]
    return jnp.clip(1.0 + 0.35 * signal + noise, 0.0, 2.0)


def touch_ends(values, key, least, top_value):
    shape = values.shape
    index_at = [jax.random.randint(jax.random.fold_in(key, axis), (), 0, shape[axis]) for axis in range(len(shape))]
    values = values.at[tuple(index_at)].set(least)
    longest = shape.index(max(shape))
    index_at[longest] = (index_at[longest] + 1) % shape[longest]
    return values.at[tuple(index_at)].set(top_value)


def setup_inputs(seed: int = 0) -> dict:
    seeds = jax.random.split(jax.random.key(seed), 3)
    dosages = draw_dosages(jax.random.fold_in(seeds[2], 71), 0)
    annotations = touch_ends(jax.random.randint(seeds[1], (VARIANTS, K), -1, 2), jax.random.fold_in(seeds[1], 1), -1, 1).astype(jnp.int32)
    return dict(dosages=dosages, annotations=annotations)


def adjust(tile, people_count):
    square = tile * tile
    return square - (1.0 - square) / (people_count - 2.0)

def reference(dosages, annotations):
    people_count = jnp.float32(dosages.shape[1])
    centre = lax.optimization_barrier(jnp.sum(dosages, axis=1)) / people_count
    spread = lax.optimization_barrier(jnp.sum(dosages * dosages, axis=1)) / people_count - centre * centre
    standard = (dosages - centre[:, None]) * lax.rsqrt(spread + 1e-06)[:, None]
    annot = annotations.astype(jnp.float32)
    num_blocks = dosages.shape[0] // B
    zblocks = standard.reshape(num_blocks, B, dosages.shape[1])
    ablocks = annot.reshape(num_blocks, B, K)
    zpadded = jnp.concatenate([zblocks, jnp.zeros((2, B, dosages.shape[1]), jnp.float32)], axis=0)
    apadded = jnp.concatenate([ablocks, jnp.zeros((2, B, K), jnp.float32)], axis=0)

    def one_block(block_index):
        own_z = lax.dynamic_index_in_dim(zpadded, block_index, 0, keepdims=False)
        own_a = lax.dynamic_index_in_dim(apadded, block_index, 0, keepdims=False)
        forward = jnp.zeros((B, K), jnp.float32)
        backs = []
        for step_ahead in range(3):
            other_z = lax.dynamic_index_in_dim(zpadded, block_index + step_ahead, 0, keepdims=False)
            other_a = lax.dynamic_index_in_dim(apadded, block_index + step_ahead, 0, keepdims=False)
            tile = jnp.dot(own_z, other_z.T, precision=lax.Precision.HIGHEST) / people_count
            adjusted = adjust(tile, people_count)
            forward = forward + jnp.dot(adjusted, other_a, precision=lax.Precision.HIGHEST)
            if step_ahead > 0:
                backs.append(jnp.dot(adjusted.T, own_a, precision=lax.Precision.HIGHEST))
        return (forward, backs[0], backs[1])
    forward, back_one, back_two = lax.map(one_block, jnp.arange(num_blocks, dtype=jnp.int32))
    result = forward
    result = result + jnp.concatenate([jnp.zeros((1, B, K), jnp.float32), back_one[:-1]], axis=0)
    result = result + jnp.concatenate([jnp.zeros((2, B, K), jnp.float32), back_two[:-2]], axis=0)
    return result.reshape(num_blocks * B, K)
```

```python
import jax
import jax.numpy as jnp
from jax import lax
from jax.sharding import PartitionSpec as P

AXES = ("genome", "people")
CHUNKS = 3


def adjust(tile, people_count):
    square = tile * tile
    return square - (1.0 - square) / (people_count - 2.0)


def mm(a, b, dims, precision):
    return lax.dot_general(a, b, (dims, ((), ())), precision=precision, preferred_element_type=jnp.float32)


def route(groups, fn):
    pairs = []
    for g in range(groups):
        for y in range(2):
            for c in range(2):
                to = fn(g, y, c)
                if to is not None and 0 <= to[0] < groups:
                    pairs.append((g * 4 + y * 2 + c, to[0] * 4 + to[1] * 2 + to[2]))
    return pairs


def local(dosages, annotations):
    groups = lax.axis_size("genome")
    rows, width = dosages.shape
    half = rows // 2
    w = half // CHUNKS
    cats = annotations.shape[1]
    people_count = jnp.float32(width * lax.axis_size("people"))
    g = lax.axis_index("genome")
    p = lax.axis_index("people")
    y, c = p // 2, p % 2

    def meets(g, c):
        return g % 2 == c

    step = lambda c: 1 - 2 * c
    routes = dict(
        x=route(groups, lambda g, y, c: (g - step(c), y, c) if not meets(g, c) else None),
        z=route(groups, lambda g, y, c: (g - 2 * step(c), y, c)),
        y=route(groups, lambda g, y, c: (g, 1 - y, c)),
        y_meet=route(groups, lambda g, y, c: (g, 1 - y, c) if meets(g, c) else None),
        pair_d=route(groups, lambda g, y, c: (g + step(c), y, 1 - c) if meets(g, c) else None),
        pair_a=route(groups, lambda g, y, c: (g + 2 * step(c), y, 1 - c)),
        pair_b=route(groups, lambda g, y, c: (g + 3 * step(c), y, 1 - c) if meets(g, c) else None),
        core=route(groups, lambda g, y, c: (g, y, 1 - c)),
    )

    kept = lambda y, c: y if c == 0 else 1 - y
    routes["res_x"] = route(groups, lambda g, y, c: (g + step(c), kept(y, c), c) if meets(g, c) else None)
    routes["res_b"] = route(groups, lambda g, y, c: (g + step(c), y, 0) if meets(g, c) and c == 1 else None)
    routes["res_z"] = route(groups, lambda g, y, c: (g + 2 * step(c), kept(y, c), c))

    def send(value, name):
        return lax.ppermute(value, AXES, routes[name])

    s_keep = jnp.where(c == 0, y, 1 - y)

    raw = dosages.reshape(2, half, width)
    raw = [raw[:, k * w:(k + 1) * w] for k in range(CHUNKS)]
    got = [(send(raw[0], "x"), send(raw[0], "z"))]

    sums = jnp.stack([jnp.sum(dosages, axis=1), jnp.sum(dosages * dosages, axis=1)])
    sums = lax.psum(sums, "people")
    centre = sums[0] / people_count
    spread = sums[1] / people_count - centre * centre
    scale = lax.rsqrt(spread + 1e-06)
    annot = annotations.astype(jnp.float32)
    side = jnp.concatenate([annot, centre.reshape(-1, cats), scale.reshape(-1, cats)], axis=0)
    side_x, side_z = send(side, "x"), send(side, "z")
    for k in range(1, CHUNKS):
        raw[k], _ = lax.optimization_barrier((raw[k], side))
        got.append((send(raw[k], "x"), send(raw[k], "z")))

    def stats(side):
        n = rows // cats
        return side[rows:rows + n].reshape(2, half), side[rows + n:].reshape(2, half)

    own = (dosages - centre[:, None]) * scale[:, None]
    stats_x, stats_z = stats(side_x), stats(side_z)

    high = lax.Precision.HIGH
    last = ((1,), (1,))
    tile0 = mm(own, own, last, high)
    tile0 = lax.psum_scatter(tile0, "people", scatter_dimension=0, tiled=True)

    def standard(value, st, k):
        centre, scale = (t[:, k * w:(k + 1) * w, None] for t in st)
        return ((value - centre) * scale).reshape(2 * w, width)

    def split(piece, keep):
        which = y if keep else 1 - y
        parts = []
        for t in range(2):
            start = (jnp.where(c == 0, which, t), 0, jnp.where(c == 0, t, which), 0)
            parts.append(lax.dynamic_slice(piece, start, (1, piece.shape[1], 1, piece.shape[3])))
        return jnp.stack(parts).reshape(2, piece.shape[1], piece.shape[3])

    zs, xs = [], []
    strips = dict(d=[], a=[], b=[])
    for k in range(CHUNKS):
        xs.append(standard(got[k][0], stats_x, k))
        zs.append(standard(got[k][1], stats_z, k))
        piece_a = mm(zs[k], own, last, high).reshape(2, w, 2, half)
        piece_d = mm(xs[k], own, last, high).reshape(2, w, 2, half)
        pieces_b = [(k, j) for j in range(k + 1)] + [(j, k) for j in range(k)]
        blocks_b = [mm(zs[i], xs[j], last, high).reshape(2, w, 2, w) for i, j in pieces_b]
        sent_a = send(split(piece_a, False), "y")
        sum_a = split(piece_a, True) + sent_a
        out = jnp.concatenate([split(piece_d, False)] + [split(b, False) for b in blocks_b], axis=2)
        mine = jnp.concatenate([split(piece_d, True)] + [split(b, True) for b in blocks_b], axis=2)
        sum_db = mine + send(out, "y_meet")
        strips["a"].append(sum_a)
        strips["d"].append(sum_db[:, :, :half])
        for n, (i, j) in enumerate(pieces_b):
            strips["b"].append(((i, j), sum_db[:, :, half + n * w:half + (n + 1) * w]))

    def choose(value, index):
        return lax.dynamic_index_in_dim(value, index, 0, keepdims=False)

    def assembled(name):
        if name == "b":
            blocks = dict(strips["b"])
            return jnp.concatenate(
                [jnp.concatenate([blocks[i, j] for j in range(CHUNKS)], axis=2) for i in range(CHUNKS)], axis=1
            )
        return jnp.concatenate(strips[name], axis=1)

    finished = {}
    for name in "dab":
        quads = assembled(name)
        back = send(choose(quads, 1 - s_keep), "pair_" + name)
        finished[name] = adjust((choose(quads, s_keep) + back.T) / people_count, people_count)

    def halves(side, index):
        return choose(side[:rows].reshape(2, half, cats), index)

    full = lax.Precision.HIGHEST
    ann_own_f = halves(annot, y)
    ann_x_s, ann_x_f = halves(side_x, s_keep), halves(side_x, y)
    ann_z_s = halves(side_z, s_keep)
    to_f = ((0,), (0,))
    to_s = ((1,), (0,))
    res_own = mm(finished["a"], ann_z_s, to_f, full) + mm(finished["d"], ann_x_s, to_f, full)
    res_b = mm(finished["b"], ann_z_s, to_f, full)
    res_x = mm(finished["d"], ann_own_f, to_s, full) + jnp.where(c == 0, res_b, 0.0)
    res_z = mm(finished["a"], ann_own_f, to_s, full) + mm(finished["b"], ann_x_f, to_s, full)
    arrived = res_own + send(res_x, "res_x") + send(res_b, "res_b") + send(res_z, "res_z")
    arrived = arrived.reshape(2, half // 2, cats)
    result = choose(arrived, c) + send(choose(arrived, 1 - c), "core")

    adjusted0 = adjust(tile0 / people_count, people_count)
    return result + mm(adjusted0, annot, to_s, full)


def solution(mesh):
    in_specs = (P("genome", "people"), P("genome", None))
    out_specs = P(("genome", "people"), None)
    return jax.shard_map(local, mesh=mesh, in_specs=in_specs, out_specs=out_specs, check_vma=False)
```

```python
import functools

import jax
import jax.numpy as jnp
from jax import lax
from jax.experimental import pallas as pl
from jax.experimental.pallas import tpu as pltpu
from jax.sharding import PartitionSpec as P

AXES = ("genome", "people")
WIDTHS = (128, 128, 64, 64)
PHASES = ((0, 1), (2, 3))
LANES = 128
F32 = jnp.float32
BF16 = jnp.bfloat16
MIB = 1024 * 1024


def adjust(tile, people_count):
    square = tile * tile
    return square - (1.0 - square) / (people_count - 2.0)


def dot(a, b, dims):
    return lax.dot_general(a, b, (dims, ((), ())), preferred_element_type=F32)


def gram(ah, al, bh, bl):
    last = ((1,), (1,))
    return dot(ah, bh, last) + (dot(ah, bl, last) + dot(al, bh, last))


def split_pair(value):
    high = value.astype(BF16)
    return high, (value - high.astype(F32)).astype(BF16)


VMEM, SMEM, HBM = pltpu.VMEM, pltpu.SMEM, pltpu.HBM


def call(kernel, ins, outs, scratch=(), room=8, flops=0, moved=0, aliases={}):
    arrays = [a if m in (None, SMEM) else pltpu.with_memory_space_constraint(a, m) for m, a in ins]
    return pl.pallas_call(
        kernel,
        out_shape=[m(s, d) if m else jax.ShapeDtypeStruct(s, d) for s, d, m in outs],
        in_specs=[pl.BlockSpec(memory_space=m or VMEM) for m, _ in ins],
        out_specs=[pl.BlockSpec(memory_space=m or VMEM) for _, _, m in outs],
        scratch_shapes=list(scratch),
        input_output_aliases=aliases,
        compiler_params=pltpu.CompilerParams(vmem_limit_bytes=room * MIB),
        cost_estimate=pl.CostEstimate(flops=flops, bytes_accessed=moved, transcendentals=0),
    )(*arrays)


class Copies:
    def __init__(self, sems):
        self.sems, self.count, self.open = sems, 0, {}

    def start(self, name, src, dst):
        copy = pltpu.make_async_copy(src, dst, self.sems.at[self.count])
        self.count += 1
        copy.start()
        self.open.setdefault(name, []).append(copy)

    def wait(self, name):
        for copy in self.open.pop(name):
            copy.wait()


class Part:
    def __init__(self, at, w):
        self.at, self.w, self.m = at, w, at // LANES
        self.last = (at + w) % LANES == 0
        self.earlier = range(self.m * LANES, at, w)
        n = self.m
        self.pieces = [(False, at, j * LANES) for j in range(n)] + [(True, at, j * LANES) for j in range(n)]
        if self.last:
            self.pieces += [(False, n * LANES + u, n * LANES) for u in range(0, LANES, w)]


def centre_rows(read, write, count, col, squares=False):
    width = read.width
    groups = width // LANES
    rows = slice(0, count)

    @pl.loop(0, count // 16)
    def _(i):
        at = pl.multiple_of(i * 16, 16)
        parts = [read(at, g) for g in range(groups)]
        while len(parts) > 1:
            parts = [a + b for a, b in zip(parts[::2], parts[1::2])]
        col[0, pl.ds(at, 16), :] = parts[0]

    spread = lambda value: jnp.broadcast_to(jnp.sum(value, axis=1, keepdims=True), (count, LANES))
    col[0, rows] = spread(col[0, rows]) * (1.0 / width)

    @pl.loop(0, count // 16)
    def _(i):
        at = pl.multiple_of(i * 16, 16)
        mean = col[0, pl.ds(at, 16), :]
        total = jnp.zeros((16, LANES), F32)
        for g in range(groups):
            value = read(at, g) - mean
            write(at, g, *split_pair(value))
            if squares:
                total += value * value
        if squares:
            col[1, pl.ds(at, 16), :] = total

    if squares:
        col[1, rows] = spread(col[1, rows])


class Rows:
    def __init__(self, ref, index, first):
        self.ref, self.index, self.first, self.width = ref, index, first, ref.shape[-1]

    def where(self, at, g):
        return *self.index, pl.ds(pl.multiple_of(self.first + at, 16), 16), slice(g * LANES, (g + 1) * LANES)

    def __call__(self, at, g):
        return self.ref[self.where(at, g)]

    def store(self, at, g, value):
        self.ref[self.where(at, g)] = value


def store_pair(high, low):
    def write(at, g, h, l):
        high.store(at, g, h)
        low.store(at, g, l)

    return write


X, Z = 0, 1


def own_kernel(parts, role, dose_hbm, *refs):
    refs = list(refs)
    take = lambda n: [refs.pop(0) for _ in range(n)]
    high_hbm, low_hbm, keep_hbm, send_hbm, moments = take(5)
    raw_hbm = take(len(parts) - 1)
    dose, high, low, tile, col, sems = refs
    c = role[1]
    blocks, size = high.shape[0], high.shape[1]
    half = blocks * LANES
    copies = Copies(sems)
    cut = lambda i: slice(i * size, (i + 1) * size)
    for i in range(blocks):
        copies.start(i, dose_hbm.at[cut(i)], dose.at[cut(i)])
    for i in range(blocks):
        copies.wait(i)
        for b in range(2):
            n = 2 * i + b
            target = [Rows(ref, (i,), b * LANES) for ref in (high, low)]
            centre_rows(Rows(dose, (), n * LANES), store_pair(*target), LANES, col, True)
            moments[n:n + 1] = col[0].T[0:1]
            moments[2 * blocks + n:2 * blocks + n + 1] = col[1].T[0:1]
        copies.start("out", high.at[i], high_hbm.at[i])
        copies.start("out", low.at[i], low_hbm.at[i])
    for part, there in zip(parts[1:], raw_hbm):
        for a in range(2):
            first = a * half + part.at
            copies.start("out", dose.at[first:first + part.w], there.at[a])

    @pl.loop(0, blocks)
    def _(i):
        at_i = pl.ds(pl.multiple_of(i * size, size), size)

        @pl.loop(0, i + 1)
        def _(j):
            at_j = pl.ds(pl.multiple_of(j * size, size), size)
            tile[at_i, at_j] = gram(high[i], low[i], high[j], low[j])

    for i in range(blocks):
        for j in range(i):
            tile[cut(j), cut(i)] = tile[cut(i), cut(j)].T
    quarter = half // 2
    for chip in range(2):
        for core, there in ((c, keep_hbm), (1 - c, send_hbm)):
            first = pl.multiple_of((2 * chip + core) * quarter, quarter)
            copies.start("out", tile.at[pl.ds(first, quarter)], there.at[chip])
    copies.wait("out")


def chunk_kernel(part, first, role, raw_z, raw_x, own_h_hbm, own_l_hbm, *refs):
    if not first:
        refs = refs[2:]
    outs, refs = refs[:4], refs[4:]
    high, low, strips, squares, left_h, left_l, col, own_h, own_l, keep_a, send_a, keep_db, send_db, sems = refs
    y, c = role[0], role[1]
    w, m = part.w, part.m
    off = part.at - m * LANES
    blocks = own_h.shape[0]
    half = blocks * LANES

    def own_copies(i):
        return [pltpu.make_async_copy(there.at[i], here.at[i], sems.at[i, n])
                for n, (there, here) in enumerate(((own_h_hbm, own_h), (own_l_hbm, own_l)))]

    for i in range(blocks):
        for copy in own_copies(i):
            copy.start()
    for name, raw in ((X, raw_x), (Z, raw_z)):
        for a in range(2):
            target = [Rows(ref, (name, m), a * LANES + off) for ref in (high, low)]
            also = [Rows(ref, (), (2 * name + a) * w) for ref in (left_h, left_l)]

            def write(at, g, h, l, target=target, also=also):
                store_pair(*target)(at, g, h, l)
                store_pair(*also)(at, g, h, l)

            centre_rows(Rows(raw, (a,), 0), write, w, col)

    @pl.loop(0, blocks)
    def _(i):
        for copy in own_copies(i):
            copy.wait()
        strips[i] = gram(left_h[...], left_l[...], own_h[i], own_l[i])

    if m:
        @pl.loop(0, 2 * m)
        def _(t):
            turned = t >= m
            at = pl.ds(pl.multiple_of(jnp.where(turned, X, Z) * 2 * w, 2 * w), 2 * w)
            right = jnp.where(turned, Z, X)
            j = jnp.where(turned, t - m, t)
            squares[t, 0:2 * w] = gram(left_h[at], left_l[at], high[right, j], low[right, j])
    if part.last:
        squares[2 * m] = gram(high[Z, m], low[Z, m], high[X, m], low[X, m])

    def rows(at, count):
        return pl.ds(pl.multiple_of(at, 16), count)

    def lanes(j):
        return pl.ds(pl.multiple_of(j * LANES, LANES), LANES)

    copies = Copies(sems.at[blocks])
    for which, out_a, out_db in ((1 - y, send_a, send_db), (y, keep_a, keep_db)):
        for t in range(2):
            s, f = jnp.where(c == 0, which, t), jnp.where(c == 0, t, which)
            for name, out in ((Z, out_a), (X, out_db)):
                for j in range(blocks):
                    group = f * blocks + j
                    at = rows((2 * name + s) * w, w)
                    out[t, :, j * LANES:(j + 1) * LANES] = strips[group // 2, at, lanes(group % 2)]
            at = half
            for b in range(2 * m):
                i, j = (f, s) if b >= m else (s, f)
                out_db[t, :, at:at + LANES] = squares[b, rows(i * w, w), lanes(j)]
                at += LANES
            if part.last:
                for u in range(0, LANES, w):
                    out_db[t, :, at:at + LANES] = squares[2 * m, rows(s * LANES + u, w), lanes(f)]
                    at += LANES
    for here, there in zip((keep_a, send_a, keep_db, send_db), outs):
        copies.start("out", here, there)
    copies.wait("out")


def load_sums(copies, t, parts, ins, held):
    for k, _ in enumerate(parts):
        for i in range(4):
            copies.start("sums", ins[k][i].at[t], held[k][i])


def sum_kernel(parts, role, *refs):
    refs = list(refs)
    take = lambda n: [refs.pop(0) for _ in range(n)]
    ins = [take(4) for _ in parts]
    out_a, out_d, out_b = take(3)
    held = [take(4) for _ in parts]
    y, c = role[0], role[1]
    copies = Copies(*refs)
    load_sums(copies, jnp.where(c == 0, 1 - y, y), parts, ins, held)
    copies.wait("sums")
    row, row_b = 0, 0
    for part, (keep_a, got_a, keep_db, got_db) in zip(parts, held):
        half, w = keep_a.shape[1], part.w
        out_a[row:row + w] = keep_a[...] + got_a[...]
        out_d[row:row + w] = keep_db[:, :half] + got_db[:, :half]
        for i in range(len(part.pieces)):
            cut = slice(half + i * LANES, half + (i + 1) * LANES)
            out_b[row_b + i * w:row_b + (i + 1) * w] = keep_db[:, cut] + got_db[:, cut]
        row += w
        row_b += w * len(part.pieces)


def correlation(tile, offsets_r, scale_r, offsets_c, scale_c, width, people_count):
    between = lax.dot_general(
        offsets_r, offsets_c, (((0,), (0,)), ((), ())), precision=lax.Precision.HIGHEST, preferred_element_type=F32
    )
    column = jnp.broadcast_to(scale_r, (8, scale_r.shape[1])).T[:, 0:1]
    return (tile + width * between) * column * scale_c / people_count


def annotated(tile, annot, dims):
    high, low = split_pair(tile)
    annot = annot.astype(BF16)
    return dot(high, annot, dims) + dot(low, annot, dims)


TO_F, TO_S = ((0,), (0,)), ((1,), (0,))


def diagonal_kernel(width, people_count, tile, tile_pair, stats_rows, stats, annot, out):
    corr = correlation(
        tile[...] + tile_pair[...], stats_rows[0:8], stats_rows[8:9], stats[0:8], stats[8:9], width, people_count
    )
    out[...] = annotated(adjust(corr, people_count), annot[...], TO_S)


def final_kernel(width, people_count, phases, role, *refs):
    refs = list(refs)
    take = lambda n: [refs.pop(0) for _ in range(n)]
    every = [part for parts in phases for part in parts]
    ins = [take(4) for _ in every]
    data = [(parts, take(3)) for parts in phases]
    own, x, z = take(2), take(2), take(2)
    res_own, res_x, res_b, res_z = take(4)
    quad, turned_quad = take(2)
    held = [take(4) for _ in every]
    y, c = role[0], role[1]
    half = quad.shape[0]
    s_keep = jnp.where(c == 0, y, 1 - y)
    copies = Copies(*refs)
    load_sums(copies, s_keep, every, ins, held)
    copies.wait("sums")

    def half_of(block, h):
        rows = pl.ds(pl.multiple_of(h * half, half), half)
        return block[0][rows, :], block[1][0:8, rows], block[1][8:9, rows]

    def fill(n, s_side, f_side):
        if n == 2:
            quad[...] = jnp.zeros_like(quad)
            turned_quad[...] = jnp.zeros_like(turned_quad)
        for part, (keep_a, got_a, keep_db, got_db) in zip(every, held):
            rows = slice(part.at, part.at + part.w)
            if n == 0:
                quad[rows] = keep_a[...] + got_a[...]
            elif n == 1:
                quad[rows] = keep_db[:, :half] + got_db[:, :half]
            else:
                for i, (turned, row, at) in enumerate(part.pieces):
                    cut = slice(half + i * LANES, half + (i + 1) * LANES)
                    mine = turned_quad if turned else quad
                    mine[row:row + part.w, at:at + LANES] += keep_db[:, cut] + got_db[:, cut]
        for parts, got in data:
            if n < 2:
                turned_quad[parts[0].at:parts[-1].at + parts[-1].w] = got[n][...]
                continue
            cut = 0
            for part in parts:
                for turned, row, at in part.pieces:
                    theirs = quad if turned else turned_quad
                    theirs[row:row + part.w, at:at + LANES] += got[2][cut:cut + part.w]
                    cut += part.w
        corr = correlation(quad[...] + turned_quad[...].T, *s_side[1:], *f_side[1:], width, people_count)
        return adjust(corr, people_count)

    own_f, x_f = half_of(own, y), half_of(x, y)
    x_s, z_s = half_of(x, s_keep), half_of(z, s_keep)
    adj = fill(0, z_s, own_f)
    res_own[...] = annotated(adj, z_s[0], TO_F)
    res_z[...] = annotated(adj, own_f[0], TO_S)
    adj = fill(1, x_s, own_f)
    res_own[...] += annotated(adj, x_s[0], TO_F)
    res_x[...] = annotated(adj, own_f[0], TO_S)
    adj = fill(2, z_s, x_f)
    back = annotated(adj, z_s[0], TO_F)
    res_b[...] = back
    res_x[...] += jnp.where(c == 0, back, 0.0)
    res_z[...] += annotated(adj, x_f[0], TO_S)


def route(groups, fn):
    pairs = []
    for g in range(groups):
        for y in range(2):
            for c in range(2):
                to = fn(g, y, c)
                if to is not None and 0 <= to[0] < groups:
                    pairs.append((g * 4 + y * 2 + c, to[0] * 4 + to[1] * 2 + to[2]))
    return pairs


def local(dosages, annotations):
    groups = lax.axis_size("genome")
    rows, width = dosages.shape
    half = rows // 2
    assert sum(WIDTHS) == half
    parts = [Part(sum(WIDTHS[:k]), w) for k, w in enumerate(WIDTHS)]
    cats = annotations.shape[1]
    total = width * lax.axis_size("people")
    people_count = jnp.float32(total)
    p = lax.axis_index("people")
    y, c = p // 2, p % 2
    role = jnp.stack([y, c]).astype(jnp.int32)

    def meets(g, c):
        return g % 2 == c

    step = lambda c: 1 - 2 * c
    kept = lambda y, c: y if c == 0 else 1 - y
    routes = dict(
        x=route(groups, lambda g, y, c: (g - step(c), y, c) if not meets(g, c) else None),
        z=route(groups, lambda g, y, c: (g - 2 * step(c), y, c)),
        y=route(groups, lambda g, y, c: (g, 1 - y, c)),
        y_meet=route(groups, lambda g, y, c: (g, 1 - y, c) if meets(g, c) else None),
        pair_d=route(groups, lambda g, y, c: (g + step(c), y, 1 - c) if meets(g, c) else None),
        pair_a=route(groups, lambda g, y, c: (g + 2 * step(c), y, 1 - c)),
        pair_b=route(groups, lambda g, y, c: (g + 3 * step(c), y, 1 - c) if meets(g, c) else None),
        core=route(groups, lambda g, y, c: (g, y, 1 - c)),
        res_x=route(groups, lambda g, y, c: (g + step(c), kept(y, c), c) if meets(g, c) else None),
        res_b=route(groups, lambda g, y, c: (g + step(c), y, 0) if meets(g, c) and c == 1 else None),
        res_z=route(groups, lambda g, y, c: (g + 2 * step(c), kept(y, c), c)),
    )

    def send(value, name):
        return lax.ppermute(value, AXES, routes[name])

    raw_0 = dosages.reshape(2, half, width)[:, :parts[0].w]
    raw = [raw_0]
    stage = lax.optimization_barrier

    def send_block(k):
        return send(raw[k], "x"), send(raw[k], "z")

    col = VMEM((2, LANES, LANES), F32)
    stack = (rows // (2 * LANES), 2 * LANES, width)
    wide = (2, *stack)
    dma = pltpu.SemaphoreType.DMA

    def run_chunk(k, got, own, old):
        part = parts[k]
        w, n_b = part.w, len(part.pieces) * LANES
        shapes = [(2, w, half)] * 2 + [(2, w, half + n_b)] * 2
        size = 2 * LANES
        *outs, high, low = call(
            functools.partial(chunk_kernel, part, k == 0),
            [(SMEM, role), (None, got[1]), (None, got[0])] + [(HBM, t) for t in own] + [(VMEM, t) for t in old],
            [(s, F32, HBM) for s in shapes] + [(wide, BF16, VMEM)] * 2,
            [VMEM((stack[0], 4 * w, size), F32), VMEM((2 * part.m + 1, size, size), F32)]
            + [VMEM((4 * w, width), BF16)] * 2 + [col] + [VMEM(stack, BF16)] * 2
            + [VMEM(s, F32) for s in shapes] + [dma((stack[0] + 1, 4))],
            room=24, flops=1, moved=1,
            aliases={5: 4, 6: 5} if k else {},
        )
        return outs, (high, low)

    def send_pair(outs):
        return outs[0], send(outs[1], "y"), outs[2], send(outs[3], "y_meet")

    def held(part):
        n_b = len(part.pieces) * LANES
        return [VMEM((part.w, half), F32)] * 2 + [VMEM((part.w, half + n_b), F32)] * 2

    def run_sum(chunk):
        phase = [parts[k] for k in chunk]
        n_rows = sum(part.w for part in phase)
        shapes = [(n_rows, half)] * 2 + [(sum(part.w * len(part.pieces) for part in phase), LANES)]
        outs = call(
            functools.partial(sum_kernel, phase), [(SMEM, role)] + [(HBM, t) for k in chunk for t in pairs[k]],
            [(s, F32, None) for s in shapes], [t for part in phase for t in held(part)] + [dma((4 * len(phase),))],
            room=10, flops=n_rows * half, moved=12 * n_rows * half,
        )
        return [send(v, n) for v, n in zip(outs, ("pair_a", "pair_d", "pair_b"))]

    got = send_block(0)
    shared = ((2, rows // 4, rows), F32, HBM)
    outs = call(
        functools.partial(own_kernel, parts), [(SMEM, role), (HBM, dosages)],
        [(stack, BF16, HBM)] * 2 + [shared] * 2 + [((2 * rows // LANES, LANES), F32, None)]
        + [((2, part.w, width), F32, HBM) for part in parts[1:]],
        [VMEM((rows, width), F32)] + [VMEM(stack, BF16)] * 2 + [VMEM((rows, rows), F32), col, dma((24,))],
        room=24, flops=4 * rows * rows * width, moved=4 * rows * width,
    )
    own, keep_0, send_0, moments, raw = outs[:2], outs[2], outs[3], outs[4], [raw_0, *outs[5:]]
    own, keep_0, send_0, moments, raw = stage((own, keep_0, send_0, moments, raw))

    both = keep_0 + send(send_0, "core")
    pick = lambda value, i: lax.dynamic_index_in_dim(value, i, 0, keepdims=False)
    tile0_own, tile0_send = pick(both, y), pick(both, 1 - y)

    moments = moments.reshape(1, 2, rows)
    moments = jnp.concatenate([moments, send(moments, "core")])
    moments = jnp.concatenate([moments, send(moments, "y")])
    centre = jnp.sum(moments[:, 0], axis=0) / moments.shape[0]
    offsets = moments[:, 0] - centre
    spread = (jnp.sum(moments[:, 1], axis=0) + width * jnp.sum(offsets * offsets, axis=0)) / people_count
    scale = lax.rsqrt(spread + 1e-06)
    annot = annotations.astype(F32)
    stats = jnp.concatenate([offsets, jnp.zeros((8 - offsets.shape[0], rows), F32), scale[None]], axis=0)
    side = jnp.concatenate([annot, stats.reshape(-1, LANES)], axis=0)
    got, own, raw, tile0_own, tile0_send, annot, stats, side = stage(
        (got, own, raw, tile0_own, tile0_send, annot, stats, side)
    )

    pairs, old = [], []
    n_parts = len(parts)
    tile0_came = send(tile0_send, "y")
    for k in range(n_parts):
        coming = send_block(k + 1) if k + 1 < n_parts else ()
        if k == n_parts - 1:
            side = [send(side, name) for name in "xz"]
        outs, old = run_chunk(k, got, own, old)
        pair = send_pair(outs)
        if k:
            last = pairs.pop()
            got, raw, old, last, own, side = stage((coming, raw, old, last, own, side))
            pairs.append(last)
        else:
            got, raw, old, own, side, tile0_came = stage((coming, raw, old, own, side, tile0_came))
        pairs.append(pair)
    tile0 = tile0_own, tile0_came
    came = side
    pairs[:3], _ = stage((pairs[:3], old))
    received = [run_sum(chunk) for chunk in PHASES]
    sides = [(annot, stats)] + [(t[:rows], t[rows:].reshape(stats.shape)) for t in came]

    phases = [[parts[k] for k in chunk] for chunk in PHASES]
    res = ((half, cats), F32, None)
    res_own, res_x, res_b, res_z = call(
        functools.partial(final_kernel, float(width), float(total), phases),
        [(SMEM, role)] + [(HBM, t) for pair in pairs for t in pair]
        + [(None, t) for group in received + sides for t in group],
        [res] * 4, [VMEM((half, half), F32)] * 2 + [t for part in parts for t in held(part)] + [dma((4 * n_parts,))],
        room=16, flops=24 * half * half * cats, moved=32 * half * half,
    )
    stats_rows = lax.dynamic_slice_in_dim(stats, p * (rows // 4), rows // 4, 1)
    (res_0,) = call(
        functools.partial(diagonal_kernel, float(width), float(total)),
        [(None, t) for t in (*tile0, stats_rows, stats, annot)], [((rows // 4, cats), F32, None)],
        flops=4 * rows * rows * cats, moved=rows * rows,
    )
    arrived = res_own + send(res_x, "res_x") + send(res_b, "res_b") + send(res_z, "res_z")
    arrived = arrived.reshape(2, half // 2, cats)
    choose = lambda index: lax.dynamic_index_in_dim(arrived, index, 0, keepdims=False)
    return choose(c) + send(choose(1 - c), "core") + res_0


def solution(mesh):
    in_specs = (P("genome", "people"), P("genome", None))
    out_specs = P(("genome", "people"), None)
    return jax.shard_map(local, mesh=mesh, in_specs=in_specs, out_specs=out_specs, check_vma=False)
```

```python
import functools

import jax
import jax.numpy as jnp
from jax import lax
from jax.experimental import pallas as pl
from jax.experimental.pallas import tpu as pltpu
from jax.sharding import PartitionSpec as P

AXES = ("genome", "people")
WIDTHS = (128, 128, 128)
EARLY = 2
LANES = 128
F32 = jnp.float32
BF16 = jnp.bfloat16
MIB = 1024 * 1024


def adjust(tile, people_count):
    square = tile * tile
    return square - (1.0 - square) / (people_count - 2.0)


def dot(a, b, dims):
    return lax.dot_general(a, b, (dims, ((), ())), preferred_element_type=F32)


def gram(ah, al, bh, bl):
    last = ((1,), (1,))
    return dot(ah, bh, last) + (dot(ah, bl, last) + dot(al, bh, last))


def split_pair(value):
    high = value.astype(BF16)
    return high, (value - high.astype(F32)).astype(BF16)


VMEM, SMEM, HBM = pltpu.VMEM, pltpu.SMEM, pltpu.HBM


def call(kernel, ins, outs, scratch=(), room=8, flops=0, moved=0, aliases={}):
    arrays = [a if m in (None, SMEM) else pltpu.with_memory_space_constraint(a, m) for m, a in ins]
    return pl.pallas_call(
        kernel,
        out_shape=[m(s, d) if m else jax.ShapeDtypeStruct(s, d) for s, d, m in outs],
        in_specs=[pl.BlockSpec(memory_space=m or VMEM) for m, _ in ins],
        out_specs=[pl.BlockSpec(memory_space=m or VMEM) for _, _, m in outs],
        scratch_shapes=list(scratch),
        input_output_aliases=aliases,
        compiler_params=pltpu.CompilerParams(vmem_limit_bytes=room * MIB),
        cost_estimate=pl.CostEstimate(flops=flops, bytes_accessed=moved, transcendentals=0),
    )(*arrays)


class Copies:
    def __init__(self, sems):
        self.sems, self.count, self.open = sems, 0, {}

    def start(self, name, src, dst):
        copy = pltpu.make_async_copy(src, dst, self.sems.at[self.count])
        self.count += 1
        copy.start()
        self.open.setdefault(name, []).append(copy)

    def wait(self, name):
        for copy in self.open.pop(name):
            copy.wait()


class Part:
    def __init__(self, at, w):
        self.at, self.w, self.m = at, w, at // LANES
        self.last = (at + w) % LANES == 0
        self.earlier = range(self.m * LANES, at, w)
        n = self.m
        self.pieces = [(False, at, j * LANES) for j in range(n)] + [(True, at, j * LANES) for j in range(n)]
        if self.last:
            self.pieces += [(False, n * LANES + u, n * LANES) for u in range(0, LANES, w)]


def centre_rows(read, write, count, col, squares=False):
    width = read.width
    groups = width // LANES
    rows = slice(0, count)

    @pl.loop(0, count // 16)
    def _(i):
        at = pl.multiple_of(i * 16, 16)
        parts = [read(at, g) for g in range(groups)]
        while len(parts) > 1:
            parts = [a + b for a, b in zip(parts[::2], parts[1::2])]
        col[0, pl.ds(at, 16), :] = parts[0]

    spread = lambda value: jnp.broadcast_to(jnp.sum(value, axis=1, keepdims=True), (count, LANES))
    col[0, rows] = spread(col[0, rows]) * (1.0 / width)

    @pl.loop(0, count // 16)
    def _(i):
        at = pl.multiple_of(i * 16, 16)
        mean = col[0, pl.ds(at, 16), :]
        total = jnp.zeros((16, LANES), F32)
        for g in range(groups):
            value = read(at, g) - mean
            write(at, g, *split_pair(value))
            if squares:
                total += value * value
        if squares:
            col[1, pl.ds(at, 16), :] = total

    if squares:
        col[1, rows] = spread(col[1, rows])


class Rows:
    def __init__(self, ref, index, first):
        self.ref, self.index, self.first, self.width = ref, index, first, ref.shape[-1]

    def where(self, at, g):
        return *self.index, pl.ds(pl.multiple_of(self.first + at, 16), 16), slice(g * LANES, (g + 1) * LANES)

    def __call__(self, at, g):
        return self.ref[self.where(at, g)]

    def store(self, at, g, value):
        self.ref[self.where(at, g)] = value


def store_pair(high, low):
    def write(at, g, h, l):
        high.store(at, g, h)
        low.store(at, g, l)

    return write


X, Z = 0, 1


def own_kernel(parts, role, dose_hbm, *refs):
    refs = list(refs)
    take = lambda n: [refs.pop(0) for _ in range(n)]
    high_hbm, low_hbm, keep_hbm, send_hbm, moments = take(5)
    raw_hbm = take(len(parts) - 1)
    dose, high, low, tile, col, sems = refs
    c = role[1]
    blocks, size = high.shape[0], high.shape[1]
    half = blocks * LANES
    copies = Copies(sems)
    cut = lambda i: slice(i * size, (i + 1) * size)
    for i in range(blocks):
        copies.start(i, dose_hbm.at[cut(i)], dose.at[cut(i)])
    for i in range(blocks):
        copies.wait(i)
        for b in range(2):
            n = 2 * i + b
            target = [Rows(ref, (i,), b * LANES) for ref in (high, low)]
            centre_rows(Rows(dose, (), n * LANES), store_pair(*target), LANES, col, True)
            moments[n:n + 1] = col[0].T[0:1]
            moments[2 * blocks + n:2 * blocks + n + 1] = col[1].T[0:1]
        copies.start("out", high.at[i], high_hbm.at[i])
        copies.start("out", low.at[i], low_hbm.at[i])
    for part, there in zip(parts[1:], raw_hbm):
        for a in range(2):
            first = a * half + part.at
            copies.start("out", dose.at[first:first + part.w], there.at[a])

    @pl.loop(0, blocks)
    def _(i):
        at_i = pl.ds(pl.multiple_of(i * size, size), size)

        @pl.loop(0, i + 1)
        def _(j):
            at_j = pl.ds(pl.multiple_of(j * size, size), size)
            tile[at_i, at_j] = gram(high[i], low[i], high[j], low[j])

    for i in range(blocks):
        for j in range(i):
            tile[cut(j), cut(i)] = tile[cut(i), cut(j)].T
    quarter = half // 2
    for chip in range(2):
        for core, there in ((c, keep_hbm), (1 - c, send_hbm)):
            first = pl.multiple_of((2 * chip + core) * quarter, quarter)
            copies.start("out", tile.at[pl.ds(first, quarter)], there.at[chip])
    copies.wait("out")


def chunk_kernel(part, name, first, role, raw, own_h, own_l, *refs):
    if not first:
        refs = refs[2:]
    keep_hbm, send_hbm, high, low, *refs = refs
    if first:
        own_hbm, (own_h, own_l), refs = (own_h, own_l), refs[:2], refs[2:]
    strips, squares, keep, send, col, sems = refs
    y, c = role[0], role[1]
    w, m = part.w, part.m
    blocks = own_h.shape[0]
    half = blocks * LANES
    assert w == LANES and part.last

    def own_copies(i):
        return [pltpu.make_async_copy(there.at[i], here.at[i], sems.at[i, n])
                for n, (there, here) in enumerate(zip(own_hbm, (own_h, own_l)))]

    if first:
        for i in range(blocks):
            for copy in own_copies(i):
                copy.start()
    for a in range(2):
        target = [Rows(ref, (name, m), a * LANES) for ref in (high, low)]
        centre_rows(Rows(raw, (a,), 0), store_pair(*target), w, col)

    @pl.loop(0, blocks)
    def _(i):
        if first:
            for copy in own_copies(i):
                copy.wait()
        strips[i] = gram(high[name, m], low[name, m], own_h[i], own_l[i])

    n_b = len(part.pieces) if name == X else 0
    if n_b:
        @pl.loop(0, n_b)
        def _(t):
            turned = (t >= m) & (t < 2 * m)
            left, right = jnp.where(turned, X, Z), jnp.where(turned, Z, X)
            j = jnp.where(t == 2 * m, m, jnp.where(turned, t - m, t))
            squares[t] = gram(high[left, m], low[left, m], high[right, j], low[right, j])

    def rows(i):
        return pl.ds(pl.multiple_of(i * LANES, LANES), LANES)

    copies = Copies(sems.at[blocks])
    for which, out, there in ((1 - y, send, send_hbm), (y, keep, keep_hbm)):
        for t in range(2):
            s, f = jnp.where(c == 0, which, t), jnp.where(c == 0, t, which)
            for j in range(blocks):
                group = f * blocks + j
                out[t, :, j * LANES:(j + 1) * LANES] = strips[group // 2, rows(s), rows(group % 2)]
            at = half
            for b in range(n_b):
                i, j = (f, s) if m <= b < 2 * m else (s, f)
                out[t, :, at:at + LANES] = squares[b, rows(i), rows(j)]
                at += LANES
        copies.start("out", out, there)
    copies.wait("out")


def load_sums(copies, t, ins, held):
    for there, here in zip(ins, held):
        copies.start("sums", there.at[t], here)


def sum_kernel(names, parts, role, *refs):
    refs = list(refs)
    take = lambda n: [refs.pop(0) for _ in range(n)]
    n = 2 * sum(strip in names for strip in "ad")
    ins = take(n * len(parts))
    outs = take(len(names))
    held = take(n * len(parts))
    y, c = role[0], role[1]
    copies = Copies(*refs)
    load_sums(copies, jnp.where(c == 0, 1 - y, y), ins, held)
    copies.wait("sums")
    row, row_b = 0, 0
    for part in parts:
        w = part.w
        if "a" in names:
            keep, got = held.pop(0), held.pop(0)
            outs[0][row:row + w] = keep[...] + got[...]
        if "d" in names:
            keep, got = held.pop(0), held.pop(0)
            out_d, out_b = outs[-2:]
            half = out_d.shape[1]
            out_d[row:row + w] = keep[:, :half] + got[:, :half]
            for i in range(len(part.pieces)):
                cut = slice(half + i * LANES, half + (i + 1) * LANES)
                out_b[row_b + i * w:row_b + (i + 1) * w] = keep[:, cut] + got[:, cut]
        row += w
        row_b += w * len(part.pieces)


def correlation(tile, offsets_r, scale_r, offsets_c, scale_c, width, people_count):
    between = lax.dot_general(
        offsets_r, offsets_c, (((0,), (0,)), ((), ())), precision=lax.Precision.HIGHEST, preferred_element_type=F32
    )
    column = jnp.broadcast_to(scale_r, (8, scale_r.shape[1])).T[:, 0:1]
    return (tile + width * between) * column * scale_c / people_count


def annotated(tile, annot, dims):
    high, low = split_pair(tile)
    annot = annot.astype(BF16)
    return dot(high, annot, dims) + dot(low, annot, dims)


TO_F, TO_S = ((0,), (0,)), ((1,), (0,))


def diagonal_kernel(width, people_count, tile, tile_pair, stats_rows, stats, annot, out):
    corr = correlation(
        tile[...] + tile_pair[...], stats_rows[0:8], stats_rows[8:9], stats[0:8], stats[8:9], width, people_count
    )
    out[...] = annotated(adjust(corr, people_count), annot[...], TO_S)


def final_kernel(width, people_count, name, phases, role, *refs):
    refs = list(refs)
    take = lambda n: [refs.pop(0) for _ in range(n)]
    every = [part for parts in phases for part in parts]
    is_a = name == "a"
    ins = take(2 * len(every))
    came = [take(1 if is_a else 2) for _ in phases]
    own, x, z = take(3)
    before = [] if is_a else take(2)
    res = take(2 if is_a else 4)
    quad, turned_quad = take(2)
    held = take(2 * len(every))
    y, c = role[0], role[1]
    half = quad.shape[0]
    s_keep = jnp.where(c == 0, y, 1 - y)
    copies = Copies(*refs)
    load_sums(copies, s_keep, ins, held)
    sums = list(zip(every, held[::2], held[1::2]))

    def half_of(block, h):
        rows = pl.ds(pl.multiple_of(h * half, half), half)
        first = [2 * half + pl.multiple_of((h * (half // LANES) + j) * 16, 16) for j in range(half // LANES)]
        part = lambda more: jnp.concatenate([block[pl.ds(at + more, 8), :] for at in first], axis=1)
        return block[rows, :], part(0), part(8)[0:1]

    def finish(s_side, f_side):
        corr = correlation(quad[...] + turned_quad[...].T, *s_side[1:], *f_side[1:], width, people_count)
        return adjust(corr, people_count)

    def strips(s_side, f_side):
        for part, keep, got in sums:
            quad[part.at:part.at + part.w] = keep[:, :half] + got[:, :half]
        for parts, got in zip(phases, came):
            turned_quad[parts[0].at:parts[-1].at + parts[-1].w] = got[0][...]
        return finish(s_side, f_side)

    def squares(s_side, f_side):
        quad[...] = jnp.zeros_like(quad)
        turned_quad[...] = jnp.zeros_like(turned_quad)
        for part, keep, got in sums:
            for i, (turned, row, at) in enumerate(part.pieces):
                cut = slice(half + i * LANES, half + (i + 1) * LANES)
                mine = turned_quad if turned else quad
                mine[row:row + part.w, at:at + LANES] += keep[:, cut] + got[:, cut]
        for parts, got in zip(phases, came):
            cut = 0
            for part in parts:
                for turned, row, at in part.pieces:
                    theirs = quad if turned else turned_quad
                    theirs[row:row + part.w, at:at + LANES] += got[1][cut:cut + part.w]
                    cut += part.w
        return finish(s_side, f_side)

    own_f = half_of(own, y)
    copies.wait("sums")
    if is_a:
        z_s = half_of(z, s_keep)
        adj = strips(z_s, own_f)
        res[0][...] = annotated(adj, z_s[0], TO_F)
        res[1][...] = annotated(adj, own_f[0], TO_S)
        return
    res_own, res_x, res_b, res_z = res
    x_s, x_f, z_s = half_of(x, s_keep), half_of(x, y), half_of(z, s_keep)
    adj = strips(x_s, own_f)
    res_own[...] = before[0][...] + annotated(adj, x_s[0], TO_F)
    back_x = annotated(adj, own_f[0], TO_S)
    adj = squares(z_s, x_f)
    back = annotated(adj, z_s[0], TO_F)
    res_b[...] = back
    res_x[...] = back_x + jnp.where(c == 0, back, 0.0)
    res_z[...] = before[1][...] + annotated(adj, x_f[0], TO_S)


def route(groups, fn):
    pairs = []
    for g in range(groups):
        for y in range(2):
            for c in range(2):
                to = fn(g, y, c)
                if to is not None and 0 <= to[0] < groups:
                    pairs.append((g * 4 + y * 2 + c, to[0] * 4 + to[1] * 2 + to[2]))
    return pairs


def local(dosages, annotations):
    groups = lax.axis_size("genome")
    rows, width = dosages.shape
    half = rows // 2
    assert sum(WIDTHS) == half
    parts = [Part(sum(WIDTHS[:k]), w) for k, w in enumerate(WIDTHS)]
    cats = annotations.shape[1]
    total = width * lax.axis_size("people")
    people_count = jnp.float32(total)
    p = lax.axis_index("people")
    y, c = p // 2, p % 2
    role = jnp.stack([y, c]).astype(jnp.int32)

    def meets(g, c):
        return g % 2 == c

    step = lambda c: 1 - 2 * c
    kept = lambda y, c: y if c == 0 else 1 - y
    routes = dict(
        x=route(groups, lambda g, y, c: (g - step(c), y, c) if not meets(g, c) else None),
        z=route(groups, lambda g, y, c: (g - 2 * step(c), y, c)),
        y=route(groups, lambda g, y, c: (g, 1 - y, c)),
        y_meet=route(groups, lambda g, y, c: (g, 1 - y, c) if meets(g, c) else None),
        pair_d=route(groups, lambda g, y, c: (g + step(c), y, 1 - c) if meets(g, c) else None),
        pair_a=route(groups, lambda g, y, c: (g + 2 * step(c), y, 1 - c)),
        pair_b=route(groups, lambda g, y, c: (g + 3 * step(c), y, 1 - c) if meets(g, c) else None),
        core=route(groups, lambda g, y, c: (g, y, 1 - c)),
        res_x=route(groups, lambda g, y, c: (g + step(c), kept(y, c), c) if meets(g, c) else None),
        res_b=route(groups, lambda g, y, c: (g + step(c), y, 0) if meets(g, c) and c == 1 else None),
        res_z=route(groups, lambda g, y, c: (g + 2 * step(c), kept(y, c), c)),
    )

    def send(value, name):
        return lax.ppermute(value, AXES, routes[name])

    raw_0 = dosages.reshape(2, half, width)[:, :parts[0].w]
    raw = [raw_0]
    stage = lax.optimization_barrier

    def send_block(k):
        return send(raw[k], "x"), send(raw[k], "z")

    col = VMEM((2, LANES, LANES), F32)
    stack = (rows // (2 * LANES), 2 * LANES, width)
    wide = (2, *stack)
    dma = pltpu.SemaphoreType.DMA

    def run_chunk(k, name, raw, own, old):
        part = parts[k]
        first = not old
        n_b = len(part.pieces) * (name == X)
        shape = (2, part.w, half + n_b * LANES)
        size = 2 * LANES
        keep, sent, *outs = call(
            functools.partial(chunk_kernel, part, name, first),
            [(SMEM, role), (None, raw)] + [(HBM if first else VMEM, t) for t in own] + [(VMEM, t) for t in old],
            [(shape, F32, HBM)] * 2 + [(wide, BF16, VMEM)] * 2 + ([(stack, BF16, VMEM)] * 2 if first else []),
            [VMEM((stack[0], size, size), F32), VMEM((max(n_b, 1), size, size), F32)]
            + [VMEM(shape, F32)] * 2 + [col, dma((stack[0] + 1, 4))],
            room=14, flops=12 * part.w * width * (rows + 2 * n_b * LANES), moved=12 * part.w * width,
            aliases={} if first else {4: 2, 5: 3},
        )
        return keep, sent, outs[2:] if first else own, outs[:2]

    def sums_of(names, chunk):
        arrays, room = [], []
        for k in chunk:
            n_b = len(parts[k].pieces) * LANES
            for i, n in ((0, half), (2, half + n_b)):
                if "ad"[i // 2] in names:
                    arrays += [(HBM, t) for t in pairs[k][i:i + 2]]
                    room += [VMEM((parts[k].w, n), F32)] * 2
        return arrays, room

    def run_sum(names, chunk, role):
        phase = [parts[k] for k in chunk]
        n_rows = sum(part.w for part in phase)
        arrays, held = sums_of(names, chunk)
        shapes = [(n_rows, half)] * (len(names) - ("b" in names))
        shapes += [(sum(part.w * len(part.pieces) for part in phase), LANES)] * ("b" in names)
        outs = call(
            functools.partial(sum_kernel, names, phase), [(SMEM, role)] + arrays, [(s, F32, None) for s in shapes],
            held + [dma((len(held),))], room=10, flops=n_rows * half, moved=12 * n_rows * half,
        )
        return [send(v, "pair_" + n) for v, n in zip(outs, names)]

    got = send_block(0)
    shared = ((2, rows // 4, rows), F32, HBM)
    outs = call(
        functools.partial(own_kernel, parts), [(SMEM, role), (HBM, dosages)],
        [(stack, BF16, HBM)] * 2 + [shared] * 2 + [((2 * rows // LANES, LANES), F32, None)]
        + [((2, part.w, width), F32, HBM) for part in parts[1:]],
        [VMEM((rows, width), F32)] + [VMEM(stack, BF16)] * 2 + [VMEM((rows, rows), F32), col, dma((24,))],
        room=24, flops=4 * rows * rows * width, moved=4 * rows * width,
    )
    own, keep_0, send_0, moments, raw = outs[:2], outs[2], outs[3], outs[4], [raw_0, *outs[5:]]
    own, keep_0, send_0, moments, raw = stage((own, keep_0, send_0, moments, raw))

    both = keep_0 + send(send_0, "core")
    pick = lambda value, i: lax.dynamic_index_in_dim(value, i, 0, keepdims=False)
    tile0_own, tile0_send = pick(both, y), pick(both, 1 - y)

    moments = moments.reshape(1, 2, rows)
    moments = jnp.concatenate([moments, send(moments, "core")])
    moments = jnp.concatenate([moments, send(moments, "y")])
    centre = jnp.sum(moments[:, 0], axis=0) / moments.shape[0]
    offsets = moments[:, 0] - centre
    spread = (jnp.sum(moments[:, 1], axis=0) + width * jnp.sum(offsets * offsets, axis=0)) / people_count
    scale = lax.rsqrt(spread + 1e-06)
    annot = annotations.astype(F32)
    fill = lambda n: jnp.zeros((n, rows), F32)
    stats = jnp.concatenate([offsets, fill(8 - offsets.shape[0]), scale[None], fill(7)], axis=0)
    by_block = stats.reshape(16, -1, LANES).transpose(1, 0, 2).reshape(-1, LANES)
    side = jnp.concatenate([annot, by_block], axis=0)
    got, own, raw, tile0_own, tile0_send, annot, stats, side = stage(
        (got, own, raw, tile0_own, tile0_send, annot, stats, side)
    )

    pairs, old = [], []
    n_parts = len(parts)
    last = n_parts - 1
    tile0_came = send(tile0_send, "y")
    for k in range(n_parts):
        coming = send_block(k + 1) if k < last else ()
        if k == last:
            came = [send(side, name) for name in "xz"]
        keep_a, sent, own, old = run_chunk(k, Z, got[1], own, old)
        if k == 0:
            sent, tile0_came = stage((sent, tile0_came))
        came_a = send(sent, "y")
        keep_db, sent, own, old = run_chunk(k, X, got[0], own, old)
        sent, came_a = stage((sent, came_a))
        pairs.append((keep_a, came_a, keep_db, send(sent, "y_meet")))
        if k < last:
            *held, came_db = pairs.pop()
            got, raw, old, own, pairs, held = stage((coming, raw, old, own, pairs, held))
            pairs.append((*held, came_db))
        else:
            came, old = stage((came, old))
    sides = [side, *came]
    early, late = range(EARLY), range(EARLY, n_parts)
    phases = [[parts[k] for k in chunk] for chunk in (early, late)]
    sent_early = run_sum("adb", early, role)
    stats_rows = lax.dynamic_slice_in_dim(stats, p * (rows // 4), rows // 4, 1)
    (res_0,) = call(
        functools.partial(diagonal_kernel, float(width), float(total)),
        [(None, t) for t in (tile0_own, tile0_came, stats_rows, stats, annot)], [((rows // 4, cats), F32, None)],
        flops=4 * rows * rows * cats, moved=rows * rows,
    )
    sent_late = run_sum("adb", late, stage((role, res_0))[0])

    def run_final(name, received, before, role):
        arrays, held = sums_of(name, range(n_parts))
        return call(
            functools.partial(final_kernel, float(width), float(total), name, phases),
            [(SMEM, role)] + arrays + [(None, t) for t in (*received, *sides, *before)],
            [((half, cats), F32, None)] * (2 if name == "a" else 4),
            [VMEM((half, half), F32)] * 2 + held + [dma((len(held),))],
            room=14, flops=12 * half * half * cats, moved=16 * half * half,
        )

    res_a = run_final("a", [sent_early[0], sent_late[0]], (), role)
    res_own, res_x, res_b, res_z = run_final("db", [*sent_early[1:], *sent_late[1:]], res_a, role)
    arrived = res_own + send(res_x, "res_x") + send(res_b, "res_b") + send(res_z, "res_z")
    arrived = arrived.reshape(2, half // 2, cats)
    choose = lambda index: lax.dynamic_index_in_dim(arrived, index, 0, keepdims=False)
    return choose(c) + send(choose(1 - c), "core") + res_0


def solution(mesh):
    in_specs = (P("genome", "people"), P("genome", None))
    out_specs = P(("genome", "people"), None)
    return jax.shard_map(local, mesh=mesh, in_specs=in_specs, out_specs=out_specs, check_vma=False)
```

```python
import functools

import jax
import jax.numpy as jnp
from jax import lax
from jax.experimental import pallas as pl
from jax.experimental.pallas import tpu as pltpu
from jax.sharding import PartitionSpec as P

AXES = ("genome", "people")
WIDTHS = (128, 128, 128)
EARLY = 2
LANES = 128
F32 = jnp.float32
BF16 = jnp.bfloat16
MIB = 1024 * 1024


def adjust(tile, people_count):
    square = tile * tile
    return square - (1.0 - square) / (people_count - 2.0)


def dot(a, b, dims):
    return lax.dot_general(a, b, (dims, ((), ())), preferred_element_type=F32)


def gram(ah, al, bh, bl):
    last = ((1,), (1,))
    return dot(ah, bh, last) + (dot(ah, bl, last) + dot(al, bh, last))


def split_pair(value):
    high = value.astype(BF16)
    return high, (value - high.astype(F32)).astype(BF16)


VMEM, SMEM, HBM = pltpu.VMEM, pltpu.SMEM, pltpu.HBM


def call(kernel, ins, outs, scratch=(), room=8, flops=0, moved=0, aliases={}):
    arrays = [a if m in (None, SMEM) else pltpu.with_memory_space_constraint(a, m) for m, a in ins]
    return pl.pallas_call(
        kernel,
        out_shape=[m(s, d) if m else jax.ShapeDtypeStruct(s, d) for s, d, m in outs],
        in_specs=[pl.BlockSpec(memory_space=m or VMEM) for m, _ in ins],
        out_specs=[pl.BlockSpec(memory_space=m or VMEM) for _, _, m in outs],
        scratch_shapes=list(scratch),
        input_output_aliases=aliases,
        compiler_params=pltpu.CompilerParams(vmem_limit_bytes=room * MIB),
        cost_estimate=pl.CostEstimate(flops=flops, bytes_accessed=moved, transcendentals=0),
    )(*arrays)


class Copies:
    def __init__(self, sems):
        self.sems, self.count, self.open = sems, 0, {}

    def start(self, name, src, dst):
        copy = pltpu.make_async_copy(src, dst, self.sems.at[self.count])
        self.count += 1
        copy.start()
        self.open.setdefault(name, []).append(copy)

    def wait(self, name):
        for copy in self.open.pop(name):
            copy.wait()


class Part:
    def __init__(self, at, w):
        self.at, self.w, self.m = at, w, at // LANES
        self.last = (at + w) % LANES == 0
        self.earlier = range(self.m * LANES, at, w)
        n = self.m
        self.pieces = [(False, at, j * LANES) for j in range(n)] + [(True, at, j * LANES) for j in range(n)]
        if self.last:
            self.pieces += [(False, n * LANES + u, n * LANES) for u in range(0, LANES, w)]


def centre_rows(read, write, count, col, squares=False):
    width = read.width
    groups = width // LANES
    rows = slice(0, count)

    @pl.loop(0, count // 16)
    def _(i):
        at = pl.multiple_of(i * 16, 16)
        parts = [read(at, g) for g in range(groups)]
        while len(parts) > 1:
            parts = [a + b for a, b in zip(parts[::2], parts[1::2])]
        col[0, pl.ds(at, 16), :] = parts[0]

    spread = lambda value: jnp.broadcast_to(jnp.sum(value, axis=1, keepdims=True), (count, LANES))
    col[0, rows] = spread(col[0, rows]) * (1.0 / width)

    @pl.loop(0, count // 16)
    def _(i):
        at = pl.multiple_of(i * 16, 16)
        mean = col[0, pl.ds(at, 16), :]
        total = jnp.zeros((16, LANES), F32)
        for g in range(groups):
            value = read(at, g) - mean
            write(at, g, *split_pair(value))
            if squares:
                total += value * value
        if squares:
            col[1, pl.ds(at, 16), :] = total

    if squares:
        col[1, rows] = spread(col[1, rows])


class Rows:
    def __init__(self, ref, index, first):
        self.ref, self.index, self.first, self.width = ref, index, first, ref.shape[-1]

    def where(self, at, g):
        return *self.index, pl.ds(pl.multiple_of(self.first + at, 16), 16), slice(g * LANES, (g + 1) * LANES)

    def __call__(self, at, g):
        return self.ref[self.where(at, g)]

    def store(self, at, g, value):
        self.ref[self.where(at, g)] = value


def store_pair(high, low):
    def write(at, g, h, l):
        high.store(at, g, h)
        low.store(at, g, l)

    return write


X, Z = 0, 1


def own_kernel(parts, dose_hbm, *refs):
    refs = list(refs)
    take = lambda n: [refs.pop(0) for _ in range(n)]
    high_hbm, low_hbm, tile_hbm, moments = take(4)
    raw_hbm = take(len(parts) - 1)
    dose, high, low, tile, col, sems = refs
    blocks, size = high.shape[0], high.shape[1]
    half = blocks * LANES
    copies = Copies(sems)
    cut = lambda i: slice(i * size, (i + 1) * size)
    for i in range(blocks):
        copies.start(i, dose_hbm.at[cut(i)], dose.at[cut(i)])
    for i in range(blocks):
        copies.wait(i)
        for b in range(2):
            n = 2 * i + b
            target = [Rows(ref, (i,), b * LANES) for ref in (high, low)]
            centre_rows(Rows(dose, (), n * LANES), store_pair(*target), LANES, col, True)
            moments[n:n + 1] = col[0].T[0:1]
            moments[2 * blocks + n:2 * blocks + n + 1] = col[1].T[0:1]
        copies.start("out", high.at[i], high_hbm.at[i])
        copies.start("out", low.at[i], low_hbm.at[i])
    for part, there in zip(parts[1:], raw_hbm):
        for a in range(2):
            first = a * half + part.at
            copies.start("out", dose.at[first:first + part.w], there.at[a])

    @pl.loop(0, blocks)
    def _(i):
        at_i = pl.ds(pl.multiple_of(i * size, size), size)

        @pl.loop(0, i + 1)
        def _(j):
            at_j = pl.ds(pl.multiple_of(j * size, size), size)
            tile[at_i, at_j] = gram(high[i], low[i], high[j], low[j])

    for i in range(blocks):
        for j in range(i):
            tile[cut(j), cut(i)] = tile[cut(i), cut(j)].T
    copies.start("out", tile, tile_hbm)
    copies.wait("out")


def chunk_kernel(part, name, first, role, raw, own_h, own_l, *refs):
    if not first:
        refs = refs[2:]
    keep_hbm, send_hbm, high, low, *refs = refs
    if first:
        own_hbm, (own_h, own_l), refs = (own_h, own_l), refs[:2], refs[2:]
    strips, squares, keep, send, col, sems = refs
    y, c = role[0], role[1]
    w, m = part.w, part.m
    blocks = own_h.shape[0]
    half = blocks * LANES
    assert w == LANES and part.last

    def own_copies(i):
        return [pltpu.make_async_copy(there.at[i], here.at[i], sems.at[i, n])
                for n, (there, here) in enumerate(zip(own_hbm, (own_h, own_l)))]

    if first:
        for i in range(blocks):
            for copy in own_copies(i):
                copy.start()
    for a in range(2):
        target = [Rows(ref, (name, m), a * LANES) for ref in (high, low)]
        centre_rows(Rows(raw, (a,), 0), store_pair(*target), w, col)

    @pl.loop(0, blocks)
    def _(i):
        if first:
            for copy in own_copies(i):
                copy.wait()
        strips[i] = gram(high[name, m], low[name, m], own_h[i], own_l[i])

    n_b = len(part.pieces) if name == X else 0
    if n_b:
        @pl.loop(0, n_b)
        def _(t):
            turned = (t >= m) & (t < 2 * m)
            left, right = jnp.where(turned, X, Z), jnp.where(turned, Z, X)
            j = jnp.where(t == 2 * m, m, jnp.where(turned, t - m, t))
            squares[t] = gram(high[left, m], low[left, m], high[right, j], low[right, j])

    def rows(i):
        return pl.ds(pl.multiple_of(i * LANES, LANES), LANES)

    copies = Copies(sems.at[blocks])
    for which, out, there in ((1 - y, send, send_hbm), (y, keep, keep_hbm)):
        for t in range(2):
            s, f = jnp.where(c == 0, which, t), jnp.where(c == 0, t, which)
            for j in range(blocks):
                group = f * blocks + j
                out[t, :, j * LANES:(j + 1) * LANES] = strips[group // 2, rows(s), rows(group % 2)]
            at = half
            for b in range(n_b):
                i, j = (f, s) if m <= b < 2 * m else (s, f)
                out[t, :, at:at + LANES] = squares[b, rows(i), rows(j)]
                at += LANES
        copies.start("out", out, there)
    copies.wait("out")


def load_sums(copies, t, ins, held):
    for there, here in zip(ins, held):
        copies.start("sums", there.at[t], here)


def sum_kernel(names, parts, role, *refs):
    refs = list(refs)
    take = lambda n: [refs.pop(0) for _ in range(n)]
    n = 2 * sum(strip in names for strip in "ad")
    ins = take(n * len(parts))
    outs = take(len(names))
    held = take(n * len(parts))
    y, c = role[0], role[1]
    copies = Copies(*refs)
    load_sums(copies, jnp.where(c == 0, 1 - y, y), ins, held)
    copies.wait("sums")
    row, row_b = 0, 0
    for part in parts:
        w = part.w
        if "a" in names:
            keep, got = held.pop(0), held.pop(0)
            outs[0][row:row + w] = keep[...] + got[...]
        if "d" in names:
            keep, got = held.pop(0), held.pop(0)
            out_d, out_b = outs[-2:]
            half = out_d.shape[1]
            out_d[row:row + w] = keep[:, :half] + got[:, :half]
            for i in range(len(part.pieces)):
                cut = slice(half + i * LANES, half + (i + 1) * LANES)
                out_b[row_b + i * w:row_b + (i + 1) * w] = keep[:, cut] + got[:, cut]
        row += w
        row_b += w * len(part.pieces)


def correlation(tile, offsets_r, scale_r, offsets_c, scale_c, width, people_count):
    between = lax.dot_general(
        offsets_r, offsets_c, (((0,), (0,)), ((), ())), precision=lax.Precision.HIGHEST, preferred_element_type=F32
    )
    column = jnp.broadcast_to(scale_r, (8, scale_r.shape[1])).T[:, 0:1]
    return (tile + width * between) * column * scale_c / people_count


def annotated(tile, annot, dims):
    high, low = split_pair(tile)
    annot = annot.astype(BF16)
    return dot(high, annot, dims) + dot(low, annot, dims)


TO_F, TO_S = ((0,), (0,)), ((1,), (0,))


def diagonal_kernel(width, people_count, tile, stats_rows, stats, annot, out):
    corr = correlation(
        tile[...], stats_rows[0:8], stats_rows[8:9], stats[0:8], stats[8:9], width, people_count
    )
    out[...] = annotated(adjust(corr, people_count), annot[...], TO_S)


def final_kernel(width, people_count, name, phases, role, *refs):
    refs = list(refs)
    take = lambda n: [refs.pop(0) for _ in range(n)]
    every = [part for parts in phases for part in parts]
    is_a = name == "a"
    ins = take(2 * len(every))
    came = [take(1 if is_a else 2) for _ in phases]
    own, x, z = take(3)
    before = [] if is_a else take(2)
    res = take(2 if is_a else 4)
    quad, turned_quad = take(2)
    held = take(2 * len(every))
    y, c = role[0], role[1]
    half = quad.shape[0]
    s_keep = jnp.where(c == 0, y, 1 - y)
    copies = Copies(*refs)
    load_sums(copies, s_keep, ins, held)
    sums = list(zip(every, held[::2], held[1::2]))

    def half_of(block, h):
        rows = pl.ds(pl.multiple_of(h * half, half), half)
        first = [2 * half + pl.multiple_of((h * (half // LANES) + j) * 16, 16) for j in range(half // LANES)]
        part = lambda more: jnp.concatenate([block[pl.ds(at + more, 8), :] for at in first], axis=1)
        return block[rows, :], part(0), part(8)[0:1]

    def finish(s_side, f_side):
        corr = correlation(quad[...] + turned_quad[...].T, *s_side[1:], *f_side[1:], width, people_count)
        return adjust(corr, people_count)

    def strips(s_side, f_side):
        for part, keep, got in sums:
            quad[part.at:part.at + part.w] = keep[:, :half] + got[:, :half]
        for parts, got in zip(phases, came):
            turned_quad[parts[0].at:parts[-1].at + parts[-1].w] = got[0][...]
        return finish(s_side, f_side)

    def squares(s_side, f_side):
        quad[...] = jnp.zeros_like(quad)
        turned_quad[...] = jnp.zeros_like(turned_quad)
        for part, keep, got in sums:
            for i, (turned, row, at) in enumerate(part.pieces):
                cut = slice(half + i * LANES, half + (i + 1) * LANES)
                mine = turned_quad if turned else quad
                mine[row:row + part.w, at:at + LANES] += keep[:, cut] + got[:, cut]
        for parts, got in zip(phases, came):
            cut = 0
            for part in parts:
                for turned, row, at in part.pieces:
                    theirs = quad if turned else turned_quad
                    theirs[row:row + part.w, at:at + LANES] += got[1][cut:cut + part.w]
                    cut += part.w
        return finish(s_side, f_side)

    own_f = half_of(own, y)
    copies.wait("sums")
    if is_a:
        z_s = half_of(z, s_keep)
        adj = strips(z_s, own_f)
        res[0][...] = annotated(adj, z_s[0], TO_F)
        res[1][...] = annotated(adj, own_f[0], TO_S)
        return
    res_own, res_x, res_b, res_z = res
    x_s, x_f, z_s = half_of(x, s_keep), half_of(x, y), half_of(z, s_keep)
    adj = strips(x_s, own_f)
    res_own[...] = before[0][...] + annotated(adj, x_s[0], TO_F)
    back_x = annotated(adj, own_f[0], TO_S)
    adj = squares(z_s, x_f)
    back = annotated(adj, z_s[0], TO_F)
    res_b[...] = back
    res_x[...] = back_x + jnp.where(c == 0, back, 0.0)
    res_z[...] = before[1][...] + annotated(adj, x_f[0], TO_S)


def route(groups, fn):
    pairs = []
    for g in range(groups):
        for y in range(2):
            for c in range(2):
                to = fn(g, y, c)
                if to is not None and 0 <= to[0] < groups:
                    pairs.append((g * 4 + y * 2 + c, to[0] * 4 + to[1] * 2 + to[2]))
    return pairs


def local(dosages, annotations):
    groups = lax.axis_size("genome")
    rows, width = dosages.shape
    half = rows // 2
    assert sum(WIDTHS) == half
    parts = [Part(sum(WIDTHS[:k]), w) for k, w in enumerate(WIDTHS)]
    cats = annotations.shape[1]
    total = width * lax.axis_size("people")
    people_count = jnp.float32(total)
    p = lax.axis_index("people")
    y, c = p // 2, p % 2
    role = jnp.stack([y, c]).astype(jnp.int32)

    def meets(g, c):
        return g % 2 == c

    step = lambda c: 1 - 2 * c
    kept = lambda y, c: y if c == 0 else 1 - y
    routes = dict(
        x=route(groups, lambda g, y, c: (g - step(c), y, c) if not meets(g, c) else None),
        z=route(groups, lambda g, y, c: (g - 2 * step(c), y, c)),
        y=route(groups, lambda g, y, c: (g, 1 - y, c)),
        y_meet=route(groups, lambda g, y, c: (g, 1 - y, c) if meets(g, c) else None),
        pair_d=route(groups, lambda g, y, c: (g + step(c), y, 1 - c) if meets(g, c) else None),
        pair_a=route(groups, lambda g, y, c: (g + 2 * step(c), y, 1 - c)),
        pair_b=route(groups, lambda g, y, c: (g + 3 * step(c), y, 1 - c) if meets(g, c) else None),
        core=route(groups, lambda g, y, c: (g, y, 1 - c)),
        res_x=route(groups, lambda g, y, c: (g + step(c), kept(y, c), c) if meets(g, c) else None),
        res_b=route(groups, lambda g, y, c: (g + step(c), y, 0) if meets(g, c) and c == 1 else None),
        res_z=route(groups, lambda g, y, c: (g + 2 * step(c), kept(y, c), c)),
    )

    def send(value, name):
        return lax.ppermute(value, AXES, routes[name])

    raw_0 = dosages.reshape(2, half, width)[:, :parts[0].w]
    raw = [raw_0]

    stage = lax.optimization_barrier

    def send_block(k):
        return send(raw[k], "x"), send(raw[k], "z")

    col = VMEM((2, LANES, LANES), F32)
    stack = (rows // (2 * LANES), 2 * LANES, width)
    wide = (2, *stack)
    dma = pltpu.SemaphoreType.DMA

    def run_chunk(k, name, raw, own, old):
        part = parts[k]
        first = not old
        n_b = len(part.pieces) * (name == X)
        shape = (2, part.w, half + n_b * LANES)
        size = 2 * LANES
        keep, sent, *outs = call(
            functools.partial(chunk_kernel, part, name, first),
            [(SMEM, role), (None, raw)] + [(HBM if first else VMEM, t) for t in own] + [(VMEM, t) for t in old],
            [(shape, F32, HBM)] * 2 + [(wide, BF16, VMEM)] * 2 + ([(stack, BF16, VMEM)] * 2 if first else []),
            [VMEM((stack[0], size, size), F32), VMEM((max(n_b, 1), size, size), F32)]
            + [VMEM(shape, F32)] * 2 + [col, dma((stack[0] + 1, 4))],
            room=14, flops=12 * part.w * width * (rows + 2 * n_b * LANES), moved=12 * part.w * width,
            aliases={} if first else {4: 2, 5: 3},
        )
        return keep, sent, outs[2:] if first else own, outs[:2]

    def sums_of(names, chunk):
        arrays, room = [], []
        for k in chunk:
            n_b = len(parts[k].pieces) * LANES
            for i, n in ((0, half), (2, half + n_b)):
                if "ad"[i // 2] in names:
                    arrays += [(HBM, t) for t in pairs[k][i:i + 2]]
                    room += [VMEM((parts[k].w, n), F32)] * 2
        return arrays, room

    def run_sum(names, chunk, role):
        phase = [parts[k] for k in chunk]
        n_rows = sum(part.w for part in phase)
        arrays, held = sums_of(names, chunk)
        shapes = [(n_rows, half)] * (len(names) - ("b" in names))
        shapes += [(sum(part.w * len(part.pieces) for part in phase), LANES)] * ("b" in names)
        outs = call(
            functools.partial(sum_kernel, names, phase), [(SMEM, role)] + arrays, [(s, F32, None) for s in shapes],
            held + [dma((len(held),))], room=10, flops=n_rows * half, moved=12 * n_rows * half,
        )
        return [send(v, "pair_" + n) for v, n in zip(outs, names)]

    got = send_block(0)
    outs = call(
        functools.partial(own_kernel, parts), [(HBM, dosages)],
        [(stack, BF16, HBM)] * 2 + [((rows, rows), F32, HBM)] + [((2 * rows // LANES, LANES), F32, None)]
        + [((2, part.w, width), F32, HBM) for part in parts[1:]],
        [VMEM((rows, width), F32)] + [VMEM(stack, BF16)] * 2 + [VMEM((rows, rows), F32), col, dma((24,))],
        room=24, flops=4 * rows * rows * width, moved=4 * rows * width,
    )
    own, tile0, moments, raw = outs[:2], outs[2], outs[3], [raw_0, *outs[4:]]
    own, tile0, moments, raw = stage((own, tile0, moments, raw))
    tile0 = lax.psum_scatter(tile0, "people", scatter_dimension=0, tiled=True)

    moments = moments.reshape(1, 2, rows)
    moments = jnp.concatenate([moments, send(moments, "core")])
    moments = jnp.concatenate([moments, send(moments, "y")])
    centre = jnp.sum(moments[:, 0], axis=0) / moments.shape[0]
    offsets = moments[:, 0] - centre
    spread = (jnp.sum(moments[:, 1], axis=0) + width * jnp.sum(offsets * offsets, axis=0)) / people_count
    scale = lax.rsqrt(spread + 1e-06)
    annot = annotations.astype(F32)
    fill = lambda n: jnp.zeros((n, rows), F32)
    stats = jnp.concatenate([offsets, fill(8 - offsets.shape[0]), scale[None], fill(7)], axis=0)
    by_block = stats.reshape(16, -1, LANES).transpose(1, 0, 2).reshape(-1, LANES)
    side = jnp.concatenate([annot, by_block], axis=0)
    got, own, annot, stats, side = stage((got, own, annot, stats, side))

    pairs, old = [], []
    n_parts = len(parts)
    last = n_parts - 1
    for k in range(n_parts):
        coming = send_block(k + 1) if k < last else ()
        if k == last:
            came = [send(side, name) for name in "xz"]
        keep_a, sent, own, old = run_chunk(k, Z, got[1], own, old)
        came_a = send(sent, "y")
        keep_db, sent, own, old = run_chunk(k, X, got[0], own, old)
        sent, came_a = stage((sent, came_a))
        if k == last:
            sent, came, pairs = stage((sent, came, pairs))
        pairs.append((keep_a, came_a, keep_db, send(sent, "y_meet")))
        if k < last:
            *held, came_db = pairs.pop()
            got, raw, old, own, pairs, held = stage((coming, raw, old, own, pairs, held))
            pairs.append((*held, came_db))
    sides = [side, *came]
    early, late = range(EARLY), range(EARLY, n_parts)
    phases = [[parts[k] for k in chunk] for chunk in (early, late)]
    sent_early = run_sum("adb", early, role)
    stats_rows = lax.dynamic_slice_in_dim(stats, p * (rows // 4), rows // 4, 1)
    (res_0,) = call(
        functools.partial(diagonal_kernel, float(width), float(total)),
        [(None, t) for t in (tile0, stats_rows, stats, annot)], [((rows // 4, cats), F32, None)],
        flops=4 * rows * rows * cats, moved=rows * rows,
    )
    sent_late = run_sum("adb", late, stage((role, res_0))[0])

    def run_final(name, received, before, role):
        arrays, held = sums_of(name, range(n_parts))
        return call(
            functools.partial(final_kernel, float(width), float(total), name, phases),
            [(SMEM, role)] + arrays + [(None, t) for t in (*received, *sides, *before)],
            [((half, cats), F32, None)] * (2 if name == "a" else 4),
            [VMEM((half, half), F32)] * 2 + held + [dma((len(held),))],
            room=14, flops=12 * half * half * cats, moved=16 * half * half,
        )

    res_a = run_final("a", [sent_early[0], sent_late[0]], (), role)
    res_own, res_x, res_b, res_z = run_final("db", [*sent_early[1:], *sent_late[1:]], res_a, role)
    arrived = res_own + send(res_x, "res_x") + send(res_b, "res_b") + send(res_z, "res_z")
    arrived = arrived.reshape(2, half // 2, cats)
    choose = lambda index: lax.dynamic_index_in_dim(arrived, index, 0, keepdims=False)
    return choose(c) + send(choose(1 - c), "core") + res_0


def solution(mesh):
    in_specs = (P("genome", "people"), P("genome", None))
    out_specs = P(("genome", "people"), None)
    return jax.shard_map(local, mesh=mesh, in_specs=in_specs, out_specs=out_specs, check_vma=False)
```

```python
import functools

import jax
import jax.numpy as jnp
from jax import lax
from jax.experimental import pallas as pl
from jax.experimental.pallas import tpu as pltpu
from jax.sharding import PartitionSpec as P

AXES = ("genome", "people")
WIDTHS = (128, 128, 128)
EARLY = 2
LANES = 128
F32 = jnp.float32
BF16 = jnp.bfloat16
MIB = 1024 * 1024


def adjust(tile, people_count):
    square = tile * tile
    return square - (1.0 - square) / (people_count - 2.0)


def dot(a, b, dims):
    return lax.dot_general(a, b, (dims, ((), ())), preferred_element_type=F32)


def gram(ah, al, bh, bl):
    last = ((1,), (1,))
    return dot(ah, bh, last) + (dot(ah, bl, last) + dot(al, bh, last))


def split_pair(value):
    high = value.astype(BF16)
    return high, (value - high.astype(F32)).astype(BF16)


VMEM, SMEM, HBM = pltpu.VMEM, pltpu.SMEM, pltpu.HBM


def call(kernel, ins, outs, scratch=(), room=8, flops=0, moved=0, aliases={}):
    arrays = [a if m in (None, SMEM) else pltpu.with_memory_space_constraint(a, m) for m, a in ins]
    return pl.pallas_call(
        kernel,
        out_shape=[m(s, d) if m else jax.ShapeDtypeStruct(s, d) for s, d, m in outs],
        in_specs=[pl.BlockSpec(memory_space=m or VMEM) for m, _ in ins],
        out_specs=[pl.BlockSpec(memory_space=m or VMEM) for _, _, m in outs],
        scratch_shapes=list(scratch),
        input_output_aliases=aliases,
        compiler_params=pltpu.CompilerParams(vmem_limit_bytes=room * MIB),
        cost_estimate=pl.CostEstimate(flops=flops, bytes_accessed=moved, transcendentals=0),
    )(*arrays)


class Copies:
    def __init__(self, sems):
        self.sems, self.count, self.open = sems, 0, {}

    def start(self, name, src, dst):
        copy = pltpu.make_async_copy(src, dst, self.sems.at[self.count])
        self.count += 1
        copy.start()
        self.open.setdefault(name, []).append(copy)

    def wait(self, name):
        for copy in self.open.pop(name):
            copy.wait()


class Part:
    def __init__(self, at, w):
        self.at, self.w, self.m = at, w, at // LANES
        self.last = (at + w) % LANES == 0
        self.earlier = range(self.m * LANES, at, w)
        n = self.m
        self.pieces = [(False, at, j * LANES) for j in range(n)] + [(True, at, j * LANES) for j in range(n)]
        if self.last:
            self.pieces += [(False, n * LANES + u, n * LANES) for u in range(0, LANES, w)]


def centre_rows(read, write, count, col, squares=False):
    width = read.width
    groups = width // LANES
    rows = slice(0, count)

    @pl.loop(0, count // 16)
    def _(i):
        at = pl.multiple_of(i * 16, 16)
        parts = [read(at, g) for g in range(groups)]
        while len(parts) > 1:
            parts = [a + b for a, b in zip(parts[::2], parts[1::2])]
        col[0, pl.ds(at, 16), :] = parts[0]

    spread = lambda value: jnp.broadcast_to(jnp.sum(value, axis=1, keepdims=True), (count, LANES))
    col[0, rows] = spread(col[0, rows]) * (1.0 / width)

    @pl.loop(0, count // 16)
    def _(i):
        at = pl.multiple_of(i * 16, 16)
        mean = col[0, pl.ds(at, 16), :]
        total = jnp.zeros((16, LANES), F32)
        for g in range(groups):
            value = read(at, g) - mean
            write(at, g, *split_pair(value))
            if squares:
                total += value * value
        if squares:
            col[1, pl.ds(at, 16), :] = total

    if squares:
        col[1, rows] = spread(col[1, rows])


class Rows:
    def __init__(self, ref, index, first):
        self.ref, self.index, self.first, self.width = ref, index, first, ref.shape[-1]

    def where(self, at, g):
        return *self.index, pl.ds(pl.multiple_of(self.first + at, 16), 16), slice(g * LANES, (g + 1) * LANES)

    def __call__(self, at, g):
        return self.ref[self.where(at, g)]

    def store(self, at, g, value):
        self.ref[self.where(at, g)] = value


def store_pair(high, low):
    def write(at, g, h, l):
        high.store(at, g, h)
        low.store(at, g, l)

    return write


X, Z = 0, 1


def own_kernel(parts, role, dose_hbm, *refs):
    refs = list(refs)
    take = lambda n: [refs.pop(0) for _ in range(n)]
    high_hbm, low_hbm, keep_hbm, send_hbm, moments = take(5)
    raw_hbm = take(len(parts) - 1)
    dose, high, low, tile, col, sems = refs
    c = role[1]
    blocks, size = high.shape[0], high.shape[1]
    half = blocks * LANES
    copies = Copies(sems)
    cut = lambda i: slice(i * size, (i + 1) * size)
    for i in range(blocks):
        copies.start(i, dose_hbm.at[cut(i)], dose.at[cut(i)])
    for i in range(blocks):
        copies.wait(i)
        for b in range(2):
            n = 2 * i + b
            target = [Rows(ref, (i,), b * LANES) for ref in (high, low)]
            centre_rows(Rows(dose, (), n * LANES), store_pair(*target), LANES, col, True)
            moments[n:n + 1] = col[0].T[0:1]
            moments[2 * blocks + n:2 * blocks + n + 1] = col[1].T[0:1]
        copies.start("out", high.at[i], high_hbm.at[i])
        copies.start("out", low.at[i], low_hbm.at[i])
    for part, there in zip(parts[1:], raw_hbm):
        for a in range(2):
            first = a * half + part.at
            copies.start("out", dose.at[first:first + part.w], there.at[a])

    @pl.loop(0, blocks)
    def _(i):
        at_i = pl.ds(pl.multiple_of(i * size, size), size)

        @pl.loop(0, i + 1)
        def _(j):
            at_j = pl.ds(pl.multiple_of(j * size, size), size)
            tile[at_i, at_j] = gram(high[i], low[i], high[j], low[j])

    for i in range(blocks):
        for j in range(i):
            tile[cut(j), cut(i)] = tile[cut(i), cut(j)].T
    quarter = half // 2
    for chip in range(2):
        for core, there in ((c, keep_hbm), (1 - c, send_hbm)):
            first = pl.multiple_of((2 * chip + core) * quarter, quarter)
            copies.start("out", tile.at[pl.ds(first, quarter)], there.at[chip])
    copies.wait("out")


def chunk_kernel(part, name, first, role, raw, own_h, own_l, *refs):
    if not first:
        refs = refs[2:]
    keep_hbm, send_hbm, high, low, *refs = refs
    if first:
        own_hbm, (own_h, own_l), refs = (own_h, own_l), refs[:2], refs[2:]
    strips, squares, keep, send, col, sems = refs
    y, c = role[0], role[1]
    w, m = part.w, part.m
    blocks = own_h.shape[0]
    half = blocks * LANES
    assert w == LANES and part.last

    def own_copies(i):
        return [pltpu.make_async_copy(there.at[i], here.at[i], sems.at[i, n])
                for n, (there, here) in enumerate(zip(own_hbm, (own_h, own_l)))]

    if first:
        for i in range(blocks):
            for copy in own_copies(i):
                copy.start()
    for a in range(2):
        target = [Rows(ref, (name, m), a * LANES) for ref in (high, low)]
        centre_rows(Rows(raw, (a,), 0), store_pair(*target), w, col)

    @pl.loop(0, blocks)
    def _(i):
        if first:
            for copy in own_copies(i):
                copy.wait()
        strips[i] = gram(high[name, m], low[name, m], own_h[i], own_l[i])

    n_b = len(part.pieces) if name == X else 0
    if n_b:
        @pl.loop(0, n_b)
        def _(t):
            turned = (t >= m) & (t < 2 * m)
            left, right = jnp.where(turned, X, Z), jnp.where(turned, Z, X)
            j = jnp.where(t == 2 * m, m, jnp.where(turned, t - m, t))
            squares[t] = gram(high[left, m], low[left, m], high[right, j], low[right, j])

    def rows(i):
        return pl.ds(pl.multiple_of(i * LANES, LANES), LANES)

    copies = Copies(sems.at[blocks])
    for which, out, there in ((1 - y, send, send_hbm), (y, keep, keep_hbm)):
        for t in range(2):
            s, f = jnp.where(c == 0, which, t), jnp.where(c == 0, t, which)
            for j in range(blocks):
                group = f * blocks + j
                out[t, :, j * LANES:(j + 1) * LANES] = strips[group // 2, rows(s), rows(group % 2)]
            at = half
            for b in range(n_b):
                i, j = (f, s) if m <= b < 2 * m else (s, f)
                out[t, :, at:at + LANES] = squares[b, rows(i), rows(j)]
                at += LANES
        copies.start("out", out, there)
    copies.wait("out")


def load_sums(copies, t, ins, held):
    for there, here in zip(ins, held):
        copies.start("sums", there.at[t], here)


def sum_kernel(names, parts, role, *refs):
    refs = list(refs)
    take = lambda n: [refs.pop(0) for _ in range(n)]
    n = 2 * sum(strip in names for strip in "ad")
    ins = take(n * len(parts))
    outs = take(len(names))
    held = take(n * len(parts))
    y, c = role[0], role[1]
    copies = Copies(*refs)
    load_sums(copies, jnp.where(c == 0, 1 - y, y), ins, held)
    copies.wait("sums")
    row, row_b = 0, 0
    for part in parts:
        w = part.w
        if "a" in names:
            keep, got = held.pop(0), held.pop(0)
            outs[0][row:row + w] = keep[...] + got[...]
        if "d" in names:
            keep, got = held.pop(0), held.pop(0)
            out_d, out_b = outs[-2:]
            half = out_d.shape[1]
            out_d[row:row + w] = keep[:, :half] + got[:, :half]
            for i in range(len(part.pieces)):
                cut = slice(half + i * LANES, half + (i + 1) * LANES)
                out_b[row_b + i * w:row_b + (i + 1) * w] = keep[:, cut] + got[:, cut]
        row += w
        row_b += w * len(part.pieces)


def correlation(tile, offsets_r, scale_r, offsets_c, scale_c, width, people_count):
    between = lax.dot_general(
        offsets_r, offsets_c, (((0,), (0,)), ((), ())), precision=lax.Precision.HIGHEST, preferred_element_type=F32
    )
    column = jnp.broadcast_to(scale_r, (8, scale_r.shape[1])).T[:, 0:1]
    return (tile + width * between) * column * scale_c / people_count


def annotated(tile, annot, dims):
    high, low = split_pair(tile)
    annot = annot.astype(BF16)
    return dot(high, annot, dims) + dot(low, annot, dims)


TO_F, TO_S = ((0,), (0,)), ((1,), (0,))


def diagonal_kernel(width, people_count, tile, tile_pair, stats_rows, stats, annot, out):
    corr = correlation(
        tile[...] + tile_pair[...], stats_rows[0:8], stats_rows[8:9], stats[0:8], stats[8:9], width, people_count
    )
    out[...] = annotated(adjust(corr, people_count), annot[...], TO_S)


def final_kernel(width, people_count, name, phases, role, *refs):
    refs = list(refs)
    take = lambda n: [refs.pop(0) for _ in range(n)]
    every = [part for parts in phases for part in parts]
    is_a = name == "a"
    ins = take(2 * len(every))
    came = [take(1 if is_a else 2) for _ in phases]
    own, x, z = take(3)
    before = [] if is_a else take(2)
    res = take(2 if is_a else 4)
    quad, turned_quad = take(2)
    held = take(2 * len(every))
    y, c = role[0], role[1]
    half = quad.shape[0]
    s_keep = jnp.where(c == 0, y, 1 - y)
    copies = Copies(*refs)
    load_sums(copies, s_keep, ins, held)
    sums = list(zip(every, held[::2], held[1::2]))

    def half_of(block, h):
        rows = pl.ds(pl.multiple_of(h * half, half), half)
        first = [2 * half + pl.multiple_of((h * (half // LANES) + j) * 16, 16) for j in range(half // LANES)]
        part = lambda more: jnp.concatenate([block[pl.ds(at + more, 8), :] for at in first], axis=1)
        return block[rows, :], part(0), part(8)[0:1]

    def finish(s_side, f_side):
        corr = correlation(quad[...] + turned_quad[...].T, *s_side[1:], *f_side[1:], width, people_count)
        return adjust(corr, people_count)

    def strips(s_side, f_side):
        for part, keep, got in sums:
            quad[part.at:part.at + part.w] = keep[:, :half] + got[:, :half]
        for parts, got in zip(phases, came):
            turned_quad[parts[0].at:parts[-1].at + parts[-1].w] = got[0][...]
        return finish(s_side, f_side)

    def squares(s_side, f_side):
        quad[...] = jnp.zeros_like(quad)
        turned_quad[...] = jnp.zeros_like(turned_quad)
        for part, keep, got in sums:
            for i, (turned, row, at) in enumerate(part.pieces):
                cut = slice(half + i * LANES, half + (i + 1) * LANES)
                mine = turned_quad if turned else quad
                mine[row:row + part.w, at:at + LANES] += keep[:, cut] + got[:, cut]
        for parts, got in zip(phases, came):
            cut = 0
            for part in parts:
                for turned, row, at in part.pieces:
                    theirs = quad if turned else turned_quad
                    theirs[row:row + part.w, at:at + LANES] += got[1][cut:cut + part.w]
                    cut += part.w
        return finish(s_side, f_side)

    own_f = half_of(own, y)
    copies.wait("sums")
    if is_a:
        z_s = half_of(z, s_keep)
        adj = strips(z_s, own_f)
        res[0][...] = annotated(adj, z_s[0], TO_F)
        res[1][...] = annotated(adj, own_f[0], TO_S)
        return
    res_own, res_x, res_b, res_z = res
    x_s, x_f, z_s = half_of(x, s_keep), half_of(x, y), half_of(z, s_keep)
    adj = strips(x_s, own_f)
    res_own[...] = before[0][...] + annotated(adj, x_s[0], TO_F)
    back_x = annotated(adj, own_f[0], TO_S)
    adj = squares(z_s, x_f)
    back = annotated(adj, z_s[0], TO_F)
    res_b[...] = back
    res_x[...] = back_x + jnp.where(c == 0, back, 0.0)
    res_z[...] = before[1][...] + annotated(adj, x_f[0], TO_S)


def route(groups, fn):
    pairs = []
    for g in range(groups):
        for y in range(2):
            for c in range(2):
                to = fn(g, y, c)
                if to is not None and 0 <= to[0] < groups:
                    pairs.append((g * 4 + y * 2 + c, to[0] * 4 + to[1] * 2 + to[2]))
    return pairs


def local(dosages, annotations):
    groups = lax.axis_size("genome")
    rows, width = dosages.shape
    half = rows // 2
    assert sum(WIDTHS) == half
    parts = [Part(sum(WIDTHS[:k]), w) for k, w in enumerate(WIDTHS)]
    cats = annotations.shape[1]
    total = width * lax.axis_size("people")
    people_count = jnp.float32(total)
    p = lax.axis_index("people")
    y, c = p // 2, p % 2
    role = jnp.stack([y, c]).astype(jnp.int32)

    def meets(g, c):
        return g % 2 == c

    step = lambda c: 1 - 2 * c
    kept = lambda y, c: y if c == 0 else 1 - y
    routes = dict(
        x=route(groups, lambda g, y, c: (g - step(c), y, c) if not meets(g, c) else None),
        z=route(groups, lambda g, y, c: (g - 2 * step(c), y, c)),
        y=route(groups, lambda g, y, c: (g, 1 - y, c)),
        y_meet=route(groups, lambda g, y, c: (g, 1 - y, c) if meets(g, c) else None),
        pair_d=route(groups, lambda g, y, c: (g + step(c), y, 1 - c) if meets(g, c) else None),
        pair_a=route(groups, lambda g, y, c: (g + 2 * step(c), y, 1 - c)),
        pair_b=route(groups, lambda g, y, c: (g + 3 * step(c), y, 1 - c) if meets(g, c) else None),
        core=route(groups, lambda g, y, c: (g, y, 1 - c)),
        res_x=route(groups, lambda g, y, c: (g + step(c), kept(y, c), c) if meets(g, c) else None),
        res_b=route(groups, lambda g, y, c: (g + step(c), y, 0) if meets(g, c) and c == 1 else None),
        res_z=route(groups, lambda g, y, c: (g + 2 * step(c), kept(y, c), c)),
    )

    def send(value, name):
        return lax.ppermute(value, AXES, routes[name])

    raw_0 = dosages.reshape(2, half, width)[:, :parts[0].w]
    raw = [raw_0]
    stage = lax.optimization_barrier

    def send_block(k):
        return send(raw[k], "x"), send(raw[k], "z")

    col = VMEM((2, LANES, LANES), F32)
    stack = (rows // (2 * LANES), 2 * LANES, width)
    wide = (2, *stack)
    dma = pltpu.SemaphoreType.DMA

    def run_chunk(k, name, raw, own, old):
        part = parts[k]
        first = not old
        n_b = len(part.pieces) * (name == X)
        shape = (2, part.w, half + n_b * LANES)
        size = 2 * LANES
        keep, sent, *outs = call(
            functools.partial(chunk_kernel, part, name, first),
            [(SMEM, role), (None, raw)] + [(HBM if first else VMEM, t) for t in own] + [(VMEM, t) for t in old],
            [(shape, F32, HBM)] * 2 + [(wide, BF16, VMEM)] * 2 + ([(stack, BF16, VMEM)] * 2 if first else []),
            [VMEM((stack[0], size, size), F32), VMEM((max(n_b, 1), size, size), F32)]
            + [VMEM(shape, F32)] * 2 + [col, dma((stack[0] + 1, 4))],
            room=14, flops=12 * part.w * width * (rows + 2 * n_b * LANES), moved=12 * part.w * width,
            aliases={} if first else {4: 2, 5: 3},
        )
        return keep, sent, outs[2:] if first else own, outs[:2]

    def sums_of(names, chunk):
        arrays, room = [], []
        for k in chunk:
            n_b = len(parts[k].pieces) * LANES
            for i, n in ((0, half), (2, half + n_b)):
                if "ad"[i // 2] in names:
                    arrays += [(HBM, t) for t in pairs[k][i:i + 2]]
                    room += [VMEM((parts[k].w, n), F32)] * 2
        return arrays, room

    def run_sum(names, chunk, role):
        phase = [parts[k] for k in chunk]
        n_rows = sum(part.w for part in phase)
        arrays, held = sums_of(names, chunk)
        shapes = [(n_rows, half)] * (len(names) - ("b" in names))
        shapes += [(sum(part.w * len(part.pieces) for part in phase), LANES)] * ("b" in names)
        outs = call(
            functools.partial(sum_kernel, names, phase), [(SMEM, role)] + arrays, [(s, F32, None) for s in shapes],
            held + [dma((len(held),))], room=10, flops=n_rows * half, moved=12 * n_rows * half,
        )
        return [send(v, "pair_" + n) for v, n in zip(outs, names)]

    got = send_block(0)
    shared = ((2, rows // 4, rows), F32, HBM)
    outs = call(
        functools.partial(own_kernel, parts), [(SMEM, role), (HBM, dosages)],
        [(stack, BF16, HBM)] * 2 + [shared] * 2 + [((2 * rows // LANES, LANES), F32, None)]
        + [((2, part.w, width), F32, HBM) for part in parts[1:]],
        [VMEM((rows, width), F32)] + [VMEM(stack, BF16)] * 2 + [VMEM((rows, rows), F32), col, dma((24,))],
        room=24, flops=4 * rows * rows * width, moved=4 * rows * width,
    )
    own, keep_0, send_0, moments, raw = outs[:2], outs[2], outs[3], outs[4], [raw_0, *outs[5:]]
    own, keep_0, send_0, moments, raw = stage((own, keep_0, send_0, moments, raw))

    both = keep_0 + send(send_0, "core")
    pick = lambda value, i: lax.dynamic_index_in_dim(value, i, 0, keepdims=False)
    tile0_own, tile0_send = pick(both, y), pick(both, 1 - y)

    moments = moments.reshape(1, 2, rows)
    moments = jnp.concatenate([moments, send(moments, "core")])
    moments, tile0_own, tile0_send = stage((moments, tile0_own, tile0_send))
    moments = jnp.concatenate([moments, send(moments, "y")])
    centre = jnp.sum(moments[:, 0], axis=0) / moments.shape[0]
    offsets = moments[:, 0] - centre
    spread = (jnp.sum(moments[:, 1], axis=0) + width * jnp.sum(offsets * offsets, axis=0)) / people_count
    scale = lax.rsqrt(spread + 1e-06)
    annot = annotations.astype(F32)
    fill = lambda n: jnp.zeros((n, rows), F32)
    stats = jnp.concatenate([offsets, fill(8 - offsets.shape[0]), scale[None], fill(7)], axis=0)
    by_block = stats.reshape(16, -1, LANES).transpose(1, 0, 2).reshape(-1, LANES)
    side = jnp.concatenate([annot, by_block], axis=0)
    got, own, tile0_own, tile0_send, annot, stats, side = stage(
        (got, own, tile0_own, tile0_send, annot, stats, side)
    )

    pairs, old = [], []
    n_parts = len(parts)
    last = n_parts - 1
    tile0_came = send(tile0_send, "y")
    for k in range(n_parts):
        coming = send_block(k + 1) if k < last else ()
        if k == last:
            came = [send(side, name) for name in "xz"]
        keep_a, sent, own, old = run_chunk(k, Z, got[1], own, old)
        if k == 0:
            sent, tile0_came = stage((sent, tile0_came))
        came_a = send(sent, "y")
        keep_db, sent, own, old = run_chunk(k, X, got[0], own, old)
        sent, came_a = stage((sent, came_a))
        if k == last:
            sent, came, pairs = stage((sent, came, pairs))
        pairs.append((keep_a, came_a, keep_db, send(sent, "y_meet")))
        if k < last:
            *held, came_db = pairs.pop()
            got, raw, old, own, pairs, held = stage((coming, raw, old, own, pairs, held))
            pairs.append((*held, came_db))
    sides = [side, *came]
    early, late = range(EARLY), range(EARLY, n_parts)
    phases = [[parts[k] for k in chunk] for chunk in (early, late)]
    sent_early = run_sum("adb", early, role)
    stats_rows = lax.dynamic_slice_in_dim(stats, p * (rows // 4), rows // 4, 1)
    (res_0,) = call(
        functools.partial(diagonal_kernel, float(width), float(total)),
        [(None, t) for t in (tile0_own, tile0_came, stats_rows, stats, annot)], [((rows // 4, cats), F32, None)],
        flops=4 * rows * rows * cats, moved=rows * rows,
    )
    sent_late = run_sum("adb", late, stage((role, res_0))[0])

    def run_final(name, received, before, role):
        arrays, held = sums_of(name, range(n_parts))
        return call(
            functools.partial(final_kernel, float(width), float(total), name, phases),
            [(SMEM, role)] + arrays + [(None, t) for t in (*received, *sides, *before)],
            [((half, cats), F32, None)] * (2 if name == "a" else 4),
            [VMEM((half, half), F32)] * 2 + held + [dma((len(held),))],
            room=14, flops=12 * half * half * cats, moved=16 * half * half,
        )

    res_a = run_final("a", [sent_early[0], sent_late[0]], (), role)
    res_own, res_x, res_b, res_z = run_final("db", [*sent_early[1:], *sent_late[1:]], res_a, role)
    arrived = res_own + send(res_x, "res_x") + send(res_b, "res_b") + send(res_z, "res_z")
    arrived = arrived.reshape(2, half // 2, cats)
    choose = lambda index: lax.dynamic_index_in_dim(arrived, index, 0, keepdims=False)
    return choose(c) + send(choose(1 - c), "core") + res_0


def solution(mesh):
    in_specs = (P("genome", "people"), P("genome", None))
    out_specs = P(("genome", "people"), None)
    return jax.shard_map(local, mesh=mesh, in_specs=in_specs, out_specs=out_specs, check_vma=False)
```
